512 devices in a mesh: gx: 16 (over z, core), yz: 32 (over y, x).
Axes of the slice: x: 4, y: 8, z: 8, core: 2. Of those that a mesh axis runs over, the one named last changes fastest.
Arguments:
- classes: int32 [128, 128, 128], P('gx', 'yz'), may hold values from 0 to 3
- contrast: float32 [4], replicated, may hold values from 0.25 to 25
- shift_x: int32 [128, 128, 7], P('gx', 'yz'), may hold values from -3 to 3, as said below
- shift_y: int32 [128, 128, 7], P('gx', 'yz'), may hold values from -3 to 3, as said below
- extent: int32 [128, 128], P('gx', 'yz'), may hold values from 1 to 8
- coarse_basis: float32 [8, 128], replicated, may hold values from -4 to 4
- stiffness: float32 [1024, 1024], replicated, may hold values from -1 to 2, as said below
Outputs:
- correction: float32 [128, 128, 8, 128], P('gx', 'yz')
The draws below stay inside these ranges and needn't reach their ends.
Inputs may be any that keep to these rules, and one draw needn't show every extreme that they name: `stiffness`: symmetric. For each element, the pairs (shift_x, shift_y) of its 7 slots are distinct positions of the box of reach 3, none of them (0, 0). `shift_y`: paired with shift_x as stated there.
All inputs are finite; a program needn't handle non-finite values.
Results may differ from the reference program's by a relative error of at most 0.0003.
Values sent between devices are 32-bit elements; how exact they have to be, the bound alone decides.
No kernel may reach another device: no remote copies, remote signals or barrier semaphores. Data moves between devices by JAX's collectives and lax.ppermute only.
A program may use at most 64 MiB of HBM per device.

```python
import math
import jax
import jax.numpy as jnp
from jax import lax

DOF = 128
SLOTS = 8
NCOL = 8
NGRP = 8
REACH = 3
NCLASS = 4
ITERS = 3
REGX = 128
REGY = 128


def box_offsets(key):
    width = 2 * REACH + 1
    cells = width * width
    keys = jax.random.split(key, REGX * REGY)

    def pick(single):
        return jax.random.permutation(single, cells - 1)[:SLOTS - 1]
    chosen = jax.vmap(pick)(keys).astype(jnp.int32)
    position = chosen + (chosen >= (cells - 1) // 2).astype(jnp.int32)
    offset_x = (position // width - REACH).reshape(REGX, REGY, SLOTS - 1)
    offset_y = (position % width - REACH).reshape(REGX, REGY, SLOTS - 1)
    return (offset_x.astype(jnp.int32), offset_y.astype(jnp.int32))


def draw_shift_x(key, part):
    offset_x, offset_y = box_offsets(key)
    return offset_x


def draw_shift_y(key, part):
    offset_x, offset_y = box_offsets(key)
    return offset_y


def draw_stiffness(key, part):
    key = jax.random.fold_in(key, 11)
    patch_order = SLOTS * DOF
    noise = jax.random.truncated_normal(key, -4.0, 4.0, (patch_order, patch_order), jnp.float32)
    coupling = (noise + noise.T) * (0.3 / math.sqrt(2.0 * patch_order))
    return jnp.eye(patch_order, dtype=jnp.float32) + coupling


def touch_ends(array, stream_key, low, largest):
    longest = array.shape.index(max(array.shape))
    spots = []
    for shift in (0, 1):
        where = [jax.random.randint(jax.random.fold_in(stream_key, axis), (), 0, length) for axis, length in enumerate(array.shape)]
        where[longest] = (where[longest] + shift) % array.shape[longest]
        spots.append(tuple(where))
    return array.at[spots[0]].set(low).at[spots[1]].set(largest)


def gaussian(rng, shape, scale, reach, kind=jnp.bfloat16):
    drawn = jax.random.normal(rng, shape, jnp.float32) * scale
    return jnp.minimum(jnp.maximum(drawn, -reach), reach).astype(kind)


def setup_inputs(seed: int = 0) -> dict:
    key_of = jax.random.split(jax.random.key(seed), 8)
    return {
        "classes": touch_ends(jax.random.randint(key_of[0], (REGX, REGY, DOF), 0, NCLASS), jax.random.fold_in(key_of[0], 1), 0, NCLASS - 1).astype(jnp.int32),
        "contrast": jnp.clip(jnp.exp(jax.random.uniform(key_of[1], (NCLASS,), jnp.float32, math.log(0.25), math.log(25.0))), 0.25, 25.0),
        "shift_x": draw_shift_x(jax.random.fold_in(key_of[7], 71), 0),
        "shift_y": draw_shift_y(jax.random.fold_in(key_of[7], 71), 0),
        "extent": touch_ends(jax.random.randint(key_of[4], (REGX, REGY), 1, SLOTS + 1), jax.random.fold_in(key_of[4], 1), 1, SLOTS).astype(jnp.int32),
        "coarse_basis": gaussian(key_of[5], (NCOL, DOF), 1.0, 4.0, jnp.float32),
        "stiffness": draw_stiffness(jax.random.fold_in(key_of[7], 71), 0),
    }


def coefficient_scale(classes, contrast):
    matches = classes[..., None] == jnp.arange(NCLASS, dtype=jnp.int32)
    return jnp.sqrt(lax.optimization_barrier(jnp.sum(jnp.where(matches, contrast, jnp.zeros_like(contrast)), axis=-1)))

def correct(slot_scale, active, coarse, stiffness):
    patches, patch_order = slot_scale.shape
    columns = coarse.shape[0]
    group_size = DOF // NGRP
    groups = patch_order // group_size

    def operate(vector):
        scaled = (slot_scale[:, None, :] * vector).reshape(patches * columns, patch_order)
        product = jnp.dot(scaled, stiffness, precision=lax.Precision.HIGHEST, preferred_element_type=jnp.float32)
        return (active * slot_scale)[:, None, :] * product.reshape(patches, columns, patch_order)
    forcing = -operate(jnp.broadcast_to(coarse, (patches, columns, patch_order)))
    inverse = 1.0 / (slot_scale * slot_scale)
    weight_sums = inverse.reshape(patches, groups, group_size).sum(-1)
    corrector = jnp.zeros_like(forcing)
    for iteration in range(ITERS):
        residual = forcing
        if iteration > 0:
            residual = forcing - operate(corrector)
        weighted = residual * inverse[:, None, :]
        multiplier = weighted.reshape(patches, columns, groups, group_size).sum(-1) / weight_sums[:, None, :]
        spread = jnp.repeat(multiplier, group_size, axis=-1)
        corrector = corrector + active[:, None, :] * (weighted - spread * inverse[:, None, :])
    return corrector

def reference(classes, contrast, shift_x, shift_y, extent, coarse_basis, stiffness):
    coef_scale = coefficient_scale(classes, contrast)
    patch_order = SLOTS * DOF
    columns = coarse_basis.shape[0]
    coarse = jnp.zeros((columns, patch_order), coef_scale.dtype).at[:, :DOF].set(coarse_basis)
    col_index = jnp.arange(REGY, dtype=jnp.int32)[:, None]

    def row_step(summed, row_index):
        index_x = jnp.concatenate([jnp.zeros((REGY, 1), jnp.int32) + row_index, (row_index + shift_x[row_index]) % REGX], axis=1)
        index_y = jnp.concatenate([col_index, (col_index + shift_y[row_index]) % REGY], axis=1)
        slot_scale = coef_scale[index_x, index_y].reshape(REGY, patch_order)
        live = jnp.arange(SLOTS, dtype=jnp.int32)[None, :] < extent[row_index][:, None]
        active = jnp.repeat(live.astype(coef_scale.dtype), DOF, axis=1)
        corrector = correct(slot_scale, active, coarse, stiffness)
        values = corrector.reshape(REGY, columns, SLOTS, DOF).transpose(0, 2, 1, 3).reshape(REGY * SLOTS, columns, DOF)
        summed = summed.at[index_x.reshape(-1), index_y.reshape(-1)].add(values)
        return (summed, None)
    initial = jnp.zeros((REGX, REGY, columns, DOF), coef_scale.dtype)
    summed, unused = lax.scan(row_step, initial, jnp.arange(REGX, dtype=jnp.int32))
    return summed
```

```python
import functools

import jax
import jax.numpy as jnp
from jax import lax
from jax.experimental import pallas as pl
from jax.experimental.pallas import tpu as pltpu
from jax.sharding import PartitionSpec as P

SLOTS = 8
NGRP = 8
REACH = 3
NCLASS = 4
ITERS = 3
BF16 = jnp.bfloat16
F32 = jnp.float32


def moved(value, axis, steps):
    count = lax.axis_size(axis)
    pairs = [(source, (source + steps) % count) for source in range(count)]
    return lax.ppermute(value, axis, pairs)


def swapped(value, axis, first):
    count = lax.axis_size(axis)
    pairs = [(k, (((k - first) ^ 1) + first) % count) for k in range(count)]
    return lax.ppermute(value, axis, pairs)


def scale_of(classes, contrast_ref):
    value = jnp.full(classes.shape, contrast_ref[0], F32)
    for k in range(1, NCLASS):
        value = jnp.where(classes == k, contrast_ref[k], value)
    return jnp.sqrt(value)


def split(value):
    high = value.astype(BF16)
    return high, (value - high.astype(F32)).astype(BF16)


def product(left, right):
    return jnp.dot(left, right, preferred_element_type=F32)


def group_ones(width, group):
    row = lax.broadcasted_iota(jnp.int32, (width, width), 0) // group
    col = lax.broadcasted_iota(jnp.int32, (width, width), 1) // group
    return jnp.where(row == col, 1.0, 0.0).astype(BF16)


def index_of(shift_x, shift_y, extent, places):
    _, col_count, row_count = shift_x.shape
    index_x = lax.broadcasted_iota(jnp.int32, shift_x.shape, 2) + shift_x
    index_y = lax.broadcasted_iota(jnp.int32, shift_y.shape, 1) + shift_y + col_count
    block = (index_y >= col_count).astype(jnp.int32) + (index_y >= 2 * col_count)
    col = index_y - block * col_count
    index = jnp.where(
        index_x < 0,
        places[3] + (block * REACH + index_x + REACH) * col_count + col,
        jnp.where(
            index_x >= row_count,
            places[4] + (block * REACH + index_x - row_count) * col_count + col,
            (block * row_count + index_x) * col_count + col,
        ),
    )
    slot = lax.broadcasted_iota(jnp.int32, shift_x.shape, 0) + 1
    return jnp.where(slot < extent, index, places[5])


def sides(near_ref, far_ref):
    even = lax.axis_index("yz") % 2 == 0
    near, far = near_ref[...], far_ref[...]
    return jnp.where(even, far, near), jnp.where(even, near, far)


def split_kernel(stiffness_ref, high_ref, low_ref):
    part = 64

    def step(k, carry):
        lines = pl.ds(pl.multiple_of(k * part, part), part)
        high_ref[lines, :], low_ref[lines, :] = split(stiffness_ref[lines, :])
        return carry

    lax.fori_loop(0, stiffness_ref.shape[0] // part, step, 0)


def pack_kernel(near_ref, far_ref, own_ref, last_out, first_out):
    left, right = sides(near_ref, far_ref)
    for k, block in enumerate((left, own_ref[...], right)):
        lines = slice(k * REACH, (k + 1) * REACH)
        last_out[lines] = block[block.shape[0] - REACH:]
        first_out[lines] = block[:REACH]


def solve_kernel(
    index_ref, contrast_ref, near_ref, own_ref, far_ref, above_ref, below_ref, coarse_ref,
    high_ref, low_ref,
    own_out, left_out, right_out, above_out, below_out,
    rows, spread, value, high, low, picture, weighted_high, weighted_low, total,
    *, row_count, col_count, dof, places,
):
    slots = SLOTS
    patches = row_count * col_count
    columns = coarse_ref.shape[0]
    own_place, empty = places[1], places[5]
    ones = group_ones(2 * dof, dof // NGRP)
    small = ones[:dof, :dof]
    rows[...] = jnp.full(rows.shape, 1.0, F32)
    left, right = sides(near_ref, far_ref)
    own_scale = scale_of(own_ref[...], contrast_ref)
    rows[pl.ds(places[0], patches), :] = scale_of(left, contrast_ref)
    rows[pl.ds(places[1], patches), :] = own_scale
    rows[pl.ds(places[2], patches), :] = scale_of(right, contrast_ref)
    for place, block in zip(places[3:], (above_ref, below_ref)):
        for x in range(block.shape[0]):
            rows[pl.ds(place + x * col_count, col_count), :] = scale_of(block[x], contrast_ref)
    inverse = 1.0 / rows[...]
    first, second = split(inverse * inverse)
    weight = product(first, small) + product(second, small)
    rows[...] = inverse * lax.rsqrt(weight)
    rows[pl.ds(empty, 8), :] = jnp.zeros((8, dof), F32)
    start = (own_scale[:, None, :] * coarse_ref[...][None]).reshape(patches * columns, dof)
    start_high, start_low = split(start)

    def tile(p, k):
        return slice(p * columns, (p + 1) * columns), slice(k * dof, (k + 1) * dof)

    def place_of(p, k):
        return index_ref[k - 1, p % col_count, p // col_count]

    for p in range(patches):
        for k in range(slots):
            row = rows[pl.ds(own_place + p if k == 0 else place_of(p, k), 1), :]
            spread[tile(p, k)] = jnp.broadcast_to(row, (columns, dof))

    pair = 2 * dof
    wide = 4 * dof
    for iteration in range(ITERS):
        for chunk in range(slots * dof // wide):
            lanes = slice(chunk * wide, (chunk + 1) * wide)
            if iteration == 0:
                image = (
                    product(start_high, high_ref[:dof, lanes])
                    + product(start_high, low_ref[:dof, lanes])
                    + product(start_low, high_ref[:dof, lanes])
                )
            else:
                source = (iteration - 1) % 2
                image = (
                    product(high[source], high_ref[:, lanes])
                    + product(high[source], low_ref[:, lanes])
                    + product(low[source], high_ref[:, lanes])
                )
            picture[:, lanes] = image
            first, second = split(spread[:, lanes] * image)
            weighted_high[:, lanes] = first
            weighted_low[:, lanes] = second
        for chunk in range(slots * dof // pair):
            lanes = slice(chunk * pair, (chunk + 1) * pair)
            factor = spread[:, lanes]
            mean = product(weighted_high[:, lanes], ones) + product(weighted_low[:, lanes], ones)
            change = jnp.where(factor > 0.0, picture[:, lanes] - factor * mean, 0.0)
            result = -change if iteration == 0 else value[:, lanes] - change
            value[:, lanes] = result
            if iteration < ITERS - 1:
                if chunk == 0:
                    result = jnp.concatenate(
                        [result[:, :dof] + start, result[:, dof:]], axis=1
                    )
                first, second = split(result)
                high[iteration % 2, :, lanes] = first
                low[iteration % 2, :, lanes] = second

    total[...] = jnp.zeros(total.shape, F32)
    for p in range(patches):
        total[own_place + p] = value[tile(p, 0)]
    for p in range(patches):
        spots = [place_of(p, k) for k in range(1, slots)]
        sums = [total[spots[k - 1]] + value[tile(p, k)] for k in range(1, slots)]
        for spot, entry in zip(spots, sums):
            total[spot] = entry
    own_out[...] = total[pl.ds(own_place, patches)].reshape(own_out.shape)
    for x in range(row_count):
        for y in range(REACH):
            left_out[x, y] = total[places[0] + x * col_count + y + col_count - REACH]
            right_out[x, y] = total[places[2] + x * col_count + y]
    for place, out in ((places[3], above_out), (places[4], below_out)):
        for x in range(REACH):
            for y in range(col_count + 2 * REACH):
                block, col = divmod(y - REACH + col_count, col_count)
                out[x, y] = total[place + (block * REACH + x) * col_count + col]


def joined_kernel(left_ref, right_ref, from_below, from_above, near_out, far_out):
    row_count, reach = left_ref.shape[:2]
    last = from_below.shape[1] - reach

    def join(source, columns, out):
        out[...] = source[...]
        out[row_count - reach:] = out[row_count - reach:] + from_below[:, columns]
        out[:reach] = out[:reach] + from_above[:, columns]

    def both(left_out, right_out):
        join(left_ref, slice(0, reach), left_out)
        join(right_ref, slice(last, last + reach), right_out)

    even = lax.axis_index("yz") % 2 == 0
    pl.when(even)(lambda: both(far_out, near_out))
    pl.when(jnp.logical_not(even))(lambda: both(near_out, far_out))


def final_kernel(
    contrast_ref, classes_ref, own_ref, near_ref, far_ref, from_below, from_above, out
):
    row_count, count = own_ref.shape[:2]
    reach = near_ref.shape[1]
    from_left, from_right = sides(near_ref, far_ref)
    middle = slice(reach, reach + count)
    inverse = 1.0 / scale_of(classes_ref[...], contrast_ref)
    out[...] = own_ref[...]
    out[:, count - reach:] = out[:, count - reach:] + from_right
    out[:, :reach] = out[:, :reach] + from_left
    out[row_count - reach:] = out[row_count - reach:] + from_below[:, middle]
    out[:reach] = out[:reach] + from_above[:, middle]
    out[...] = out[...] * inverse[:, :, None, :]


SMEM = pl.BlockSpec(memory_space=pltpu.SMEM)
VMEM = pl.BlockSpec(memory_space=pltpu.VMEM)


def grant(mebibytes):
    return pltpu.CompilerParams(vmem_limit_bytes=mebibytes * 1024 * 1024)


def shapes(*dims):
    return jax.ShapeDtypeStruct(dims, F32)


def per_device(classes, contrast, shift_x, shift_y, extent, coarse_basis, stiffness):
    row_count, col_count, dof = classes.shape
    columns = coarse_basis.shape[0]
    order = SLOTS * dof
    patches = row_count * col_count
    edge = 3 * REACH * col_count
    places = [0, patches, 2 * patches, 3 * patches]
    places += [places[3] + (edge + 7) // 8 * 8]
    places += [places[4] + (edge + 7) // 8 * 8]
    empty = places[5]

    far = swapped(classes, "yz", 1)
    near = swapped(classes, "yz", 0)

    index = index_of(
        shift_x.transpose(2, 1, 0), shift_y.transpose(2, 1, 0), extent.T, places
    )
    stiff = jax.ShapeDtypeStruct((order, order), BF16)
    stiff_high, stiff_low = pl.pallas_call(
        split_kernel,
        in_specs=[VMEM],
        out_specs=[VMEM] * 2,
        out_shape=[stiff, stiff],
        compiler_params=grant(4),
        cost_estimate=pl.CostEstimate(
            flops=2 * order * order, bytes_accessed=8 * order * order, transcendentals=0
        ),
        name="split",
    )(stiffness)
    near, far, stiff_high, stiff_low, index = lax.optimization_barrier(
        (near, far, stiff_high, stiff_low, index)
    )
    halo = jax.ShapeDtypeStruct((3 * REACH, col_count, dof), jnp.int32)
    last_rows, first_rows = pl.pallas_call(
        pack_kernel,
        in_specs=[VMEM] * 3,
        out_specs=[VMEM] * 2,
        out_shape=[halo, halo],
        compiler_params=grant(4),
        name="pack",
    )(near, far, classes)
    above = moved(last_rows, "gx", 1)
    below = moved(first_rows, "gx", -1)

    ext_cols = col_count + 2 * REACH
    whole = (row_count, col_count, columns, dof)
    own_sum, left_sum, right_sum, above_sum, below_sum = pl.pallas_call(
        functools.partial(
            solve_kernel, row_count=row_count, col_count=col_count, dof=dof, places=places
        ),
        in_specs=[SMEM, SMEM] + [VMEM] * 8,
        out_specs=[VMEM] * 5,
        out_shape=[
            shapes(*whole),
            shapes(row_count, REACH, columns, dof),
            shapes(row_count, REACH, columns, dof),
            shapes(REACH, ext_cols, columns, dof),
            shapes(REACH, ext_cols, columns, dof),
        ],
        scratch_shapes=[
            pltpu.VMEM((empty + 8, dof), F32),
            pltpu.VMEM((patches * columns, order), F32),
            pltpu.VMEM((patches * columns, order), F32),
            pltpu.VMEM((2, patches * columns, order), BF16),
            pltpu.VMEM((2, patches * columns, order), BF16),
            pltpu.VMEM((patches * columns, order), F32),
            pltpu.VMEM((patches * columns, order), BF16),
            pltpu.VMEM((patches * columns, order), BF16),
            pltpu.VMEM((empty + 1, columns, dof), F32),
        ],
        compiler_params=grant(14),
        name="solve",
    )(
        index, contrast, near.reshape(patches, dof), classes.reshape(patches, dof),
        far.reshape(patches, dof), above, below, coarse_basis, stiff_high, stiff_low,
    )

    from_below = moved(above_sum, "gx", -1)
    from_above = moved(below_sum, "gx", 1)
    side = shapes(row_count, REACH, columns, dof)
    near_sum, far_sum = pl.pallas_call(
        joined_kernel,
        in_specs=[VMEM] * 4,
        out_specs=[VMEM] * 2,
        out_shape=[side, side],
        compiler_params=grant(4),
        name="joined",
    )(left_sum, right_sum, from_below, from_above)
    far_sum = swapped(far_sum, "yz", 1)
    near_sum = swapped(near_sum, "yz", 0)
    return pl.pallas_call(
        final_kernel,
        in_specs=[SMEM] + [VMEM] * 6,
        out_specs=VMEM,
        out_shape=shapes(*whole),
        compiler_params=grant(4),
        name="final",
    )(contrast, classes, own_sum, near_sum, far_sum, from_below, from_above)


def solution(mesh):
    return jax.shard_map(
        per_device,
        mesh=mesh,
        in_specs=(
            P("gx", "yz", None),
            P(),
            P("gx", "yz", None),
            P("gx", "yz", None),
            P("gx", "yz"),
            P(),
            P(),
        ),
        out_specs=P("gx", "yz", None, None),
        check_vma=False,
    )
```

```python
import functools

import jax
import jax.numpy as jnp
from jax import lax
from jax.experimental import pallas as pl
from jax.experimental.pallas import tpu as pltpu
from jax.sharding import PartitionSpec as P

SLOTS = 8
NGRP = 8
REACH = 3
NCLASS = 4
ITERS = 3
BF16 = jnp.bfloat16
F32 = jnp.float32


def moved(value, axis, steps):
    count = lax.axis_size(axis)
    pairs = [(source, (source + steps) % count) for source in range(count)]
    return lax.ppermute(value, axis, pairs)


def swapped(value, axis, first):
    count = lax.axis_size(axis)
    pairs = [(k, (((k - first) ^ 1) + first) % count) for k in range(count)]
    return lax.ppermute(value, axis, pairs)


def scale_of(classes, contrast_ref):
    value = jnp.full(classes.shape, contrast_ref[0], F32)
    for k in range(1, NCLASS):
        value = jnp.where(classes == k, contrast_ref[k], value)
    return jnp.sqrt(value)


def split(value):
    high = value.astype(BF16)
    return high, (value - high.astype(F32)).astype(BF16)


def product(left, right):
    return jnp.dot(left, right, preferred_element_type=F32)


def group_ones(width, group):
    row = lax.broadcasted_iota(jnp.int32, (width, width), 0) // group
    col = lax.broadcasted_iota(jnp.int32, (width, width), 1) // group
    return jnp.where(row == col, 1.0, 0.0).astype(BF16)


def index_of(shift_x, shift_y, extent, places):
    _, col_count, row_count = shift_x.shape
    index_x = lax.broadcasted_iota(jnp.int32, shift_x.shape, 2) + shift_x
    index_y = lax.broadcasted_iota(jnp.int32, shift_y.shape, 1) + shift_y + col_count
    block = (index_y >= col_count).astype(jnp.int32) + (index_y >= 2 * col_count)
    col = index_y - block * col_count
    index = jnp.where(
        index_x < 0,
        places[3] + (block * REACH + index_x + REACH) * col_count + col,
        jnp.where(
            index_x >= row_count,
            places[4] + (block * REACH + index_x - row_count) * col_count + col,
            (block * row_count + index_x) * col_count + col,
        ),
    )
    slot = lax.broadcasted_iota(jnp.int32, shift_x.shape, 0) + 1
    return jnp.where(slot < extent, index, places[5])


def sides(near_ref, far_ref):
    even = lax.axis_index("yz") % 2 == 0
    near, far = near_ref[...], far_ref[...]
    return jnp.where(even, far, near), jnp.where(even, near, far)


def split_kernel(stiffness_ref, high_ref, low_ref):
    part = 64

    def step(k, carry):
        lines = pl.ds(pl.multiple_of(k * part, part), part)
        high_ref[lines, :], low_ref[lines, :] = split(stiffness_ref[lines, :])
        return carry

    lax.fori_loop(0, stiffness_ref.shape[0] // part, step, 0)


def pack_kernel(near_ref, far_ref, own_ref, last_out, first_out):
    left, right = sides(near_ref, far_ref)
    for k, block in enumerate((left, own_ref[...], right)):
        lines = slice(k * REACH, (k + 1) * REACH)
        last_out[lines] = block[block.shape[0] - REACH:]
        first_out[lines] = block[:REACH]


def solve_kernel(
    index_ref, contrast_ref, near_ref, own_ref, far_ref, above_ref, below_ref, coarse_ref,
    high_ref, low_ref,
    own_out, left_out, right_out, below_out, above_out,
    rows, spread, value, high, low, picture, weighted_high, weighted_low, total,
    *, row_count, col_count, dof, places,
):
    slots = SLOTS
    patches = row_count * col_count
    columns = coarse_ref.shape[0]
    own_place, empty = places[1], places[5]
    ones = group_ones(2 * dof, dof // NGRP)
    small = ones[:dof, :dof]
    rows[...] = jnp.full(rows.shape, 1.0, F32)
    left, right = sides(near_ref, far_ref)
    own_scale = scale_of(own_ref[...], contrast_ref)
    rows[pl.ds(places[0], patches), :] = scale_of(left, contrast_ref)
    rows[pl.ds(places[1], patches), :] = own_scale
    rows[pl.ds(places[2], patches), :] = scale_of(right, contrast_ref)
    for place, block in zip(places[3:], (above_ref, below_ref)):
        for x in range(block.shape[0]):
            rows[pl.ds(place + x * col_count, col_count), :] = scale_of(block[x], contrast_ref)
    inverse = 1.0 / rows[...]
    first, second = split(inverse * inverse)
    weight = product(first, small) + product(second, small)
    rows[...] = inverse * lax.rsqrt(weight)
    rows[pl.ds(empty, 8), :] = jnp.zeros((8, dof), F32)
    start = (own_scale[:, None, :] * coarse_ref[...][None]).reshape(patches * columns, dof)
    start_high, start_low = split(start)

    def tile(p, k):
        return slice(p * columns, (p + 1) * columns), slice(k * dof, (k + 1) * dof)

    def place_of(p, k):
        return index_ref[k - 1, p % col_count, p // col_count]

    for p in range(patches):
        for k in range(slots):
            row = rows[pl.ds(own_place + p if k == 0 else place_of(p, k), 1), :]
            spread[tile(p, k)] = jnp.broadcast_to(row, (columns, dof))

    pair = 2 * dof
    wide = 4 * dof
    for iteration in range(ITERS):
        for chunk in range(slots * dof // wide):
            lanes = slice(chunk * wide, (chunk + 1) * wide)
            if iteration == 0:
                image = (
                    product(start_high, high_ref[:dof, lanes])
                    + product(start_high, low_ref[:dof, lanes])
                    + product(start_low, high_ref[:dof, lanes])
                )
            else:
                source = (iteration - 1) % 2
                image = (
                    product(high[source], high_ref[:, lanes])
                    + product(high[source], low_ref[:, lanes])
                    + product(low[source], high_ref[:, lanes])
                )
            picture[:, lanes] = image
            first, second = split(spread[:, lanes] * image)
            weighted_high[:, lanes] = first
            weighted_low[:, lanes] = second
        for chunk in range(slots * dof // pair):
            lanes = slice(chunk * pair, (chunk + 1) * pair)
            factor = spread[:, lanes]
            mean = product(weighted_high[:, lanes], ones) + product(weighted_low[:, lanes], ones)
            change = jnp.where(factor > 0.0, picture[:, lanes] - factor * mean, 0.0)
            result = -change if iteration == 0 else value[:, lanes] - change
            value[:, lanes] = result
            if iteration < ITERS - 1:
                if chunk == 0:
                    result = jnp.concatenate(
                        [result[:, :dof] + start, result[:, dof:]], axis=1
                    )
                first, second = split(result)
                high[iteration % 2, :, lanes] = first
                low[iteration % 2, :, lanes] = second

    total[...] = jnp.zeros(total.shape, F32)
    for p in range(patches):
        total[own_place + p] = value[tile(p, 0)]
    for p in range(patches):
        spots = [place_of(p, k) for k in range(1, slots)]
        sums = [total[spots[k - 1]] + value[tile(p, k)] for k in range(1, slots)]
        for spot, entry in zip(spots, sums):
            total[spot] = entry
    own_out[...] = total[pl.ds(own_place, patches)].reshape(own_out.shape)
    for x in range(row_count):
        for y in range(REACH):
            left_out[x, y] = total[places[0] + x * col_count + y + col_count - REACH]
            right_out[x, y] = total[places[2] + x * col_count + y]
    for place, out in ((places[3], above_out), (places[4], below_out)):
        for x in range(REACH):
            for y in range(col_count + 2 * REACH):
                block, col = divmod(y - REACH + col_count, col_count)
                out[x, y] = total[place + (block * REACH + x) * col_count + col]


def joined_kernel(left_ref, right_ref, from_above, from_below, far_out, near_out):
    row_count, reach = left_ref.shape[:2]
    last = from_below.shape[1] - reach

    def join(source, columns, out):
        out[...] = source[...]
        out[row_count - reach:] = out[row_count - reach:] + from_below[:, columns]
        out[:reach] = out[:reach] + from_above[:, columns]

    def both(left_out, right_out):
        join(left_ref, slice(0, reach), left_out)
        join(right_ref, slice(last, last + reach), right_out)

    even = lax.axis_index("yz") % 2 == 0
    pl.when(even)(lambda: both(far_out, near_out))
    pl.when(jnp.logical_not(even))(lambda: both(near_out, far_out))


def final_kernel(
    contrast_ref, classes_ref, own_ref, far_ref, near_ref, from_above, from_below, out
):
    row_count, count = own_ref.shape[:2]
    reach = near_ref.shape[1]
    from_left, from_right = sides(near_ref, far_ref)
    middle = slice(reach, reach + count)
    inverse = 1.0 / scale_of(classes_ref[...], contrast_ref)
    out[...] = own_ref[...]
    out[:, count - reach:] = out[:, count - reach:] + from_right
    out[:, :reach] = out[:, :reach] + from_left
    out[row_count - reach:] = out[row_count - reach:] + from_below[:, middle]
    out[:reach] = out[:reach] + from_above[:, middle]
    out[...] = out[...] * inverse[:, :, None, :]


SMEM = pl.BlockSpec(memory_space=pltpu.SMEM)
VMEM = pl.BlockSpec(memory_space=pltpu.VMEM)


def grant(mebibytes):
    return pltpu.CompilerParams(vmem_limit_bytes=mebibytes * 1024 * 1024)


def shapes(*dims):
    return jax.ShapeDtypeStruct(dims, F32)


def per_device(classes, contrast, shift_x, shift_y, extent, coarse_basis, stiffness):
    row_count, col_count, dof = classes.shape
    columns = coarse_basis.shape[0]
    order = SLOTS * dof
    patches = row_count * col_count
    edge = 3 * REACH * col_count
    places = [0, patches, 2 * patches, 3 * patches]
    places += [places[3] + (edge + 7) // 8 * 8]
    places += [places[4] + (edge + 7) // 8 * 8]
    empty = places[5]

    far = swapped(classes, "yz", 1)
    near = swapped(classes, "yz", 0)

    index = index_of(
        shift_x.transpose(2, 1, 0), shift_y.transpose(2, 1, 0), extent.T, places
    )
    stiff = jax.ShapeDtypeStruct((order, order), BF16)
    stiff_high, stiff_low = pl.pallas_call(
        split_kernel,
        in_specs=[VMEM],
        out_specs=[VMEM] * 2,
        out_shape=[stiff, stiff],
        compiler_params=grant(4),
        cost_estimate=pl.CostEstimate(
            flops=2 * order * order, bytes_accessed=8 * order * order, transcendentals=0
        ),
        name="split",
    )(stiffness)
    near, far, stiff_high, stiff_low, index = lax.optimization_barrier(
        (near, far, stiff_high, stiff_low, index)
    )
    halo = jax.ShapeDtypeStruct((3 * REACH, col_count, dof), jnp.int32)
    last_rows, first_rows = pl.pallas_call(
        pack_kernel,
        in_specs=[VMEM] * 3,
        out_specs=[VMEM] * 2,
        out_shape=[halo, halo],
        compiler_params=grant(4),
        name="pack",
    )(near, far, classes)
    above = moved(last_rows, "gx", 1)
    below = moved(first_rows, "gx", -1)

    ext_cols = col_count + 2 * REACH
    whole = (row_count, col_count, columns, dof)
    own_sum, left_sum, right_sum, below_sum, above_sum = pl.pallas_call(
        functools.partial(
            solve_kernel, row_count=row_count, col_count=col_count, dof=dof, places=places
        ),
        in_specs=[SMEM, SMEM] + [VMEM] * 8,
        out_specs=[VMEM] * 5,
        out_shape=[
            shapes(*whole),
            shapes(row_count, REACH, columns, dof),
            shapes(row_count, REACH, columns, dof),
            shapes(REACH, ext_cols, columns, dof),
            shapes(REACH, ext_cols, columns, dof),
        ],
        scratch_shapes=[
            pltpu.VMEM((empty + 8, dof), F32),
            pltpu.VMEM((patches * columns, order), F32),
            pltpu.VMEM((patches * columns, order), F32),
            pltpu.VMEM((2, patches * columns, order), BF16),
            pltpu.VMEM((2, patches * columns, order), BF16),
            pltpu.VMEM((patches * columns, order), F32),
            pltpu.VMEM((patches * columns, order), BF16),
            pltpu.VMEM((patches * columns, order), BF16),
            pltpu.VMEM((empty + 1, columns, dof), F32),
        ],
        compiler_params=grant(14),
        name="solve",
    )(
        index, contrast, near.reshape(patches, dof), classes.reshape(patches, dof),
        far.reshape(patches, dof), above, below, coarse_basis, stiff_high, stiff_low,
    )

    from_below = moved(above_sum, "gx", -1)
    from_above = moved(below_sum, "gx", 1)
    side = shapes(row_count, REACH, columns, dof)
    far_sum, near_sum = pl.pallas_call(
        joined_kernel,
        in_specs=[VMEM] * 4,
        out_specs=[VMEM] * 2,
        out_shape=[side, side],
        compiler_params=grant(4),
        name="joined",
    )(left_sum, right_sum, from_above, from_below)
    far_sum = swapped(far_sum, "yz", 1)
    near_sum = swapped(near_sum, "yz", 0)
    return pl.pallas_call(
        final_kernel,
        in_specs=[SMEM] + [VMEM] * 6,
        out_specs=VMEM,
        out_shape=shapes(*whole),
        compiler_params=grant(4),
        name="final",
    )(contrast, classes, own_sum, far_sum, near_sum, from_above, from_below)


def solution(mesh):
    return jax.shard_map(
        per_device,
        mesh=mesh,
        in_specs=(
            P("gx", "yz", None),
            P(),
            P("gx", "yz", None),
            P("gx", "yz", None),
            P("gx", "yz"),
            P(),
            P(),
        ),
        out_specs=P("gx", "yz", None, None),
        check_vma=False,
    )
```

```python
import functools

import jax
import jax.numpy as jnp
from jax import lax
from jax.experimental import pallas as pl
from jax.experimental.pallas import tpu as pltpu
from jax.sharding import PartitionSpec as P

SLOTS = 8
NGRP = 8
REACH = 3
NCLASS = 4
ITERS = 3
BF16 = jnp.bfloat16
F32 = jnp.float32


def moved(value, axis, steps):
    count = lax.axis_size(axis)
    pairs = [(source, (source + steps) % count) for source in range(count)]
    return lax.ppermute(value, axis, pairs)


def swapped(value, axis, first):
    count = lax.axis_size(axis)
    pairs = [(k, (((k - first) ^ 1) + first) % count) for k in range(count)]
    return lax.ppermute(value, axis, pairs)


def scale_of(classes, contrast_ref):
    value = jnp.full(classes.shape, contrast_ref[0], F32)
    for k in range(1, NCLASS):
        value = jnp.where(classes == k, contrast_ref[k], value)
    return jnp.sqrt(value)


def split(value):
    high = value.astype(BF16)
    return high, (value - high.astype(F32)).astype(BF16)


def product(left, right):
    return jnp.dot(left, right, preferred_element_type=F32)


def group_ones(width, group):
    row = lax.broadcasted_iota(jnp.int32, (width, width), 0) // group
    col = lax.broadcasted_iota(jnp.int32, (width, width), 1) // group
    return jnp.where(row == col, 1.0, 0.0).astype(BF16)


def places_of(index_x, index_y, places, row_count, col_count):
    block = (index_y >= col_count).astype(jnp.int32) + (index_y >= 2 * col_count)
    col = index_y - block * col_count
    deep = 2 * REACH
    return jnp.where(
        index_x < 0,
        places[3] + (block * deep + index_x + deep) * col_count + col,
        jnp.where(
            index_x >= row_count,
            places[4] + (block * deep + index_x - row_count) * col_count + col,
            (block * row_count + index_x) * col_count + col,
        ),
    )


def sides(near_ref, far_ref):
    even = lax.axis_index("yz") % 2 == 0
    near, far = near_ref[...], far_ref[...]
    return jnp.where(even, far, near), jnp.where(even, near, far)


def prepare_kernel(
    shift_x_ref, shift_y_ref, extent_ref, classes_ref, stiffness_ref,
    own_out, info_out, down_out, up_out, high_ref, low_ref,
    shift_x, shift_y, extent, landing, arrived, *, places,
):
    parts, part = landing.shape[:2]
    small = 64

    def copy(k):
        return pltpu.make_async_copy(
            stiffness_ref.at[pl.ds(k * part, part), :], landing.at[k], arrived.at[k]
        )

    others = [
        pltpu.make_async_copy(source, target, arrived.at[parts + k])
        for k, (source, target) in enumerate((
            (shift_x_ref, shift_x), (shift_y_ref, shift_y), (extent_ref, extent),
            (classes_ref, own_out),
        ))
    ]
    for other in others:
        other.start()
    for k in range(parts):
        copy(k).start()
    for other in others:
        other.wait()
    col_count, row_count = extent.shape
    shape = shift_x.shape
    slot = lax.broadcasted_iota(jnp.int32, shape, 0) + 1
    index_x = lax.broadcasted_iota(jnp.int32, shape, 2) + shift_x[...]
    index_y = lax.broadcasted_iota(jnp.int32, shape, 1) + shift_y[...] + col_count
    live = slot < extent[...][None]
    for out, move in ((info_out, 0), (down_out, -row_count), (up_out, row_count)):
        place = places_of(index_x + move, index_y, places, row_count, col_count)
        out[0] = extent[...]
        out[1:] = jnp.where(live, place, places[5])
    for k in range(parts):
        copy(k).wait()

        def step(j, carry):
            lines = pl.ds(pl.multiple_of(k * part + j * small, small), small)
            source = pl.ds(pl.multiple_of(j * small, small), small)
            high_ref[lines, :], low_ref[lines, :] = split(landing[k, source, :])
            return carry

        lax.fori_loop(0, part // small, step, 0)


def pack_kernel(far_ref, near_ref, own_ref, down_ref, up_ref, last_out, first_out, *, bound):
    left, right = sides(near_ref, far_ref)
    deep = 2 * REACH
    for k, block in enumerate((left, own_ref[...], right)):
        lines = slice(k * deep, (k + 1) * deep)
        last_out[lines] = block[block.shape[0] - deep:]
        first_out[lines] = block[:deep]
    for info_ref, out in ((down_ref, last_out), (up_ref, first_out)):
        places = info_ref[1:]
        reached = jnp.max((places < bound).astype(jnp.int32), axis=0)
        head = 3 * deep
        count = info_ref.shape[2]
        out[head:] = jnp.zeros((out.shape[0] - head,) + out.shape[1:], jnp.int32)
        out[head, :, :count] = info_ref[0] * reached
        out[head + 1:, :, :count] = places


def solve_kernel(
    info_ref, contrast_ref, near_ref, own_ref, far_ref, above_ref, below_ref, coarse_ref,
    high_ref, low_ref,
    own_out, far_out, near_out,
    scales, rows, start, spread, value, high, low, picture, weighted_high, weighted_low, total,
    ranks, *, row_count, col_count, dof, places,
):
    slots = SLOTS
    patches = row_count * col_count
    columns = coarse_ref.shape[0]
    own_place, bound, empty = places[1], places[3], places[5]
    deep = 2 * REACH
    ones = group_ones(2 * dof, dof // NGRP)
    small = ones[:dof, :dof]
    scales[...] = jnp.full(scales.shape, 1.0, F32)
    left, right = sides(near_ref, far_ref)
    for place, block in zip(places, (left, own_ref[...], right)):
        scales[pl.ds(place, patches), :] = scale_of(block, contrast_ref)
    for place, block in zip(places[3:], (above_ref, below_ref)):
        for x in range(3 * deep):
            scales[pl.ds(place + x * col_count, col_count), :] = scale_of(block[x], contrast_ref)
    inverse = 1.0 / scales[...]
    first, second = split(inverse * inverse)
    weight = product(first, small) + product(second, small)
    rows[...] = inverse * lax.rsqrt(weight)
    rows[pl.ds(empty, 8), :] = jnp.zeros((8, dof), F32)

    elements = [(r, y) for r in range(row_count + 2 * REACH) for y in range(col_count)]

    def first_place(r, y):
        x = r - REACH
        if x < 0:
            return places[3] + (deep + x + deep) * col_count + y
        if x >= row_count:
            return places[4] + (deep + x - row_count) * col_count + y
        return own_place + x * col_count + y

    width = 6
    half = 5

    def counted(extent, counters):
        late = extent >= half
        shift = jnp.where(late, extent - half, extent) * width
        step = jnp.left_shift(jnp.int32(1), shift)
        counter = jnp.where(late, counters[1], counters[0])
        held = jnp.bitwise_and(jnp.right_shift(counter, shift), (1 << width) - 1)
        none = jnp.int32(0)
        return held, (
            counters[0] + jnp.where(late, none, step), counters[1] + jnp.where(late, step, none)
        )

    counters = (jnp.int32(0), jnp.int32(0))
    for r, y in elements:
        _, counters = counted(info_ref[0, y, r], counters)
    starts = [jnp.int32(0), jnp.int32(0)]
    longer = [None] * (slots + 1)
    before = jnp.int32(0)
    for extent in range(slots, -1, -1):
        part, shift = divmod(extent, half)
        longer[extent] = before
        starts[part] = starts[part] + jnp.left_shift(before, shift * width)
        number = jnp.right_shift(counters[part], shift * width)
        before = before + jnp.bitwise_and(number, (1 << width) - 1)
    counters = tuple(starts)
    for p, (r, y) in enumerate(elements):
        rank, counters = counted(info_ref[0, y, r], counters)
        ranks[p] = rank
    for p, (r, y) in enumerate(elements):
        lines = pl.ds(pl.multiple_of(ranks[p] * columns, columns), columns)
        place = first_place(r, y)
        start[lines, :] = scales[place:place + 1, :] * coarse_ref[...]
        for k in range(slots):
            row = rows[pl.ds(place if k == 0 else info_ref[k, y, r], 1), :]
            spread[lines, k * dof:(k + 1) * dof] = jnp.broadcast_to(row, (columns, dof))

    block_rows = high.shape[1]
    pair = 2 * dof
    wide = 2 * pair

    def solve_block(b, pairs):
        lines = pl.ds(pl.multiple_of(b * block_rows, block_rows), block_rows)
        active = pairs * pair
        begin = start[lines, :]
        begin_high, begin_low = split(begin)
        for iteration in range(ITERS):
            for base in range(0, active, wide):
                lanes = slice(base, min(base + wide, active))
                if iteration == 0:
                    image = (
                        product(begin_high, high_ref[:dof, lanes])
                        + product(begin_high, low_ref[:dof, lanes])
                        + product(begin_low, high_ref[:dof, lanes])
                    )
                else:
                    source = (iteration - 1) % 2
                    image = (
                        product(high[source, :, :active], high_ref[:active, lanes])
                        + product(high[source, :, :active], low_ref[:active, lanes])
                        + product(low[source, :, :active], high_ref[:active, lanes])
                    )
                picture[:, lanes] = image
                first, second = split(spread[lines, lanes] * image)
                weighted_high[:, lanes] = first
                weighted_low[:, lanes] = second
            for base in range(0, active, pair):
                lanes = slice(base, base + pair)
                factor = spread[lines, lanes]
                mean = product(weighted_high[:, lanes], ones)
                mean = mean + product(weighted_low[:, lanes], ones)
                change = jnp.where(factor > 0.0, picture[:, lanes] - factor * mean, 0.0)
                result = -change if iteration == 0 else value[lines, lanes] - change
                value[lines, lanes] = result
                if iteration < ITERS - 1:
                    if base == 0:
                        result = jnp.concatenate(
                            [result[:, :dof] + begin, result[:, dof:]], axis=1
                        )
                    first, second = split(result)
                    high[iteration % 2, :, lanes] = first
                    low[iteration % 2, :, lanes] = second

    def solve_step(b, carry):
        passed = b * (block_rows // columns)
        pairs = jnp.int32(0)
        for k in range(slots // 2):
            pairs = pairs + jnp.where(longer[2 * k] > passed, 1, 0)
        for k in range(1, slots // 2 + 1):
            pl.when(pairs == k)(functools.partial(solve_block, b, k))
        return carry

    lax.fori_loop(0, spread.shape[0] // block_rows, solve_step, 0)

    total[...] = jnp.zeros(total.shape, F32)

    def result_of(p, k):
        lines = pl.ds(pl.multiple_of(ranks[p] * columns, columns), columns)
        return value[lines, k * dof:(k + 1) * dof]

    for p in range(patches):
        total[0, own_place + p] = result_of(p + REACH * col_count, 0)
    count = len(elements) // 2
    for q in range(count):
        sums = []
        for part in range(2):
            p = q + part * count
            r, y = elements[p]
            for k in range(1, slots):
                spot = jnp.minimum(info_ref[k, y, r], bound)
                sums.append((part, spot, total[part, spot] + result_of(p, k)))
        for part, spot, entry in sums:
            total[part, spot] = entry
    total[0] = total[0] + total[1]
    total = total.at[0]
    own_out[...] = total[pl.ds(own_place, patches)].reshape(own_out.shape)

    def store_sides(left_out, right_out):
        for x in range(row_count):
            for y in range(REACH):
                left_out[x, y] = total[places[0] + x * col_count + y + col_count - REACH]
                right_out[x, y] = total[places[2] + x * col_count + y]

    even = lax.axis_index("yz") % 2 == 0
    pl.when(even)(lambda: store_sides(far_out, near_out))
    pl.when(jnp.logical_not(even))(lambda: store_sides(near_out, far_out))


def final_kernel(contrast_ref, classes_ref, own_ref, far_ref, near_ref, out):
    count = own_ref.shape[1]
    reach = near_ref.shape[1]
    from_left, from_right = sides(near_ref, far_ref)
    inverse = 1.0 / scale_of(classes_ref[...], contrast_ref)
    out[...] = own_ref[...]
    out[:, count - reach:] = out[:, count - reach:] + from_right
    out[:, :reach] = out[:, :reach] + from_left
    out[...] = out[...] * inverse[:, :, None, :]


SMEM = pl.BlockSpec(memory_space=pltpu.SMEM)
VMEM = pl.BlockSpec(memory_space=pltpu.VMEM)


def grant(mebibytes):
    return pltpu.CompilerParams(vmem_limit_bytes=mebibytes * 1024 * 1024)


def shapes(*dims):
    return jax.ShapeDtypeStruct(dims, F32)


def per_device(classes, contrast, shift_x, shift_y, extent, coarse_basis, stiffness):
    row_count, col_count, dof = classes.shape
    columns = coarse_basis.shape[0]
    order = SLOTS * dof
    patches = row_count * col_count
    edge = 3 * 2 * REACH * col_count
    places = [0, patches, 2 * patches, 3 * patches, 3 * patches + edge, 3 * patches + 2 * edge]
    empty = places[5]

    far = swapped(classes, "yz", 1)
    near = swapped(classes, "yz", 0)

    stiff = jax.ShapeDtypeStruct((order, order), BF16)
    ends = jax.ShapeDtypeStruct((SLOTS, col_count, row_count), jnp.int32)
    parts = 8
    turned = (SLOTS - 1, col_count, row_count)
    sources = (
        shift_x.transpose(2, 1, 0), shift_y.transpose(2, 1, 0), extent.T, classes, stiffness
    )
    own, info, down, up, stiff_high, stiff_low = pl.pallas_call(
        functools.partial(prepare_kernel, places=places),
        in_specs=[pl.BlockSpec(memory_space=pltpu.HBM)] * 5,
        out_specs=[VMEM] * 6,
        out_shape=[
            jax.ShapeDtypeStruct(classes.shape, jnp.int32), ends, ends, ends, stiff, stiff
        ],
        scratch_shapes=[
            pltpu.VMEM(turned, jnp.int32),
            pltpu.VMEM(turned, jnp.int32),
            pltpu.VMEM(turned[1:], jnp.int32),
            pltpu.VMEM((parts, order // parts, order), F32),
            pltpu.SemaphoreType.DMA((parts + 4,)),
        ],
        compiler_params=grant(8),
        cost_estimate=pl.CostEstimate(
            flops=2 * order * order, bytes_accessed=8 * order * order, transcendentals=0
        ),
        name="prepare",
    )(*(pltpu.with_memory_space_constraint(source, pltpu.HBM) for source in sources))
    far, near, own, stiff_high, stiff_low, info, down, up = lax.optimization_barrier(
        (far, near, own, stiff_high, stiff_low, info, down, up)
    )
    head = 3 * 2 * REACH
    halo = jax.ShapeDtypeStruct((head + SLOTS, col_count, dof), jnp.int32)
    last_rows, first_rows = pl.pallas_call(
        functools.partial(pack_kernel, bound=places[3]),
        in_specs=[VMEM] * 5,
        out_specs=[VMEM] * 2,
        out_shape=[halo, halo],
        compiler_params=grant(4),
        name="pack",
    )(far, near, own, down, up)
    above = moved(last_rows, "gx", 1)
    below = moved(first_rows, "gx", -1)

    info = jnp.concatenate(
        [above[head:, :, row_count - REACH:row_count], info, below[head:, :, :REACH]], axis=2
    )
    whole = (row_count, col_count, columns, dof)
    side = shapes(row_count, REACH, columns, dof)
    total_rows = (row_count + 2 * REACH) * col_count * columns
    block_rows = total_rows // 2
    own_sum, far_sum, near_sum = pl.pallas_call(
        functools.partial(
            solve_kernel, row_count=row_count, col_count=col_count, dof=dof, places=places
        ),
        in_specs=[SMEM, SMEM] + [VMEM] * 8,
        out_specs=[VMEM] * 3,
        out_shape=[shapes(*whole), side, side],
        scratch_shapes=[
            pltpu.VMEM((empty + 8, dof), F32),
            pltpu.VMEM((empty + 8, dof), F32),
            pltpu.VMEM((total_rows, dof), F32),
            pltpu.VMEM((total_rows, order), F32),
            pltpu.VMEM((total_rows, order), F32),
            pltpu.VMEM((2, block_rows, order), BF16),
            pltpu.VMEM((2, block_rows, order), BF16),
            pltpu.VMEM((block_rows, order), F32),
            pltpu.VMEM((block_rows, order), BF16),
            pltpu.VMEM((block_rows, order), BF16),
            pltpu.VMEM((2, places[3] + 1, columns, dof), F32),
            pltpu.SMEM((64,), jnp.int32),
        ],
        compiler_params=grant(16),
        name="solve",
    )(
        info, contrast, near.reshape(patches, dof), own.reshape(patches, dof),
        far.reshape(patches, dof), above, below, coarse_basis, stiff_high, stiff_low,
    )
    far_sum = swapped(far_sum, "yz", 1)
    near_sum = swapped(near_sum, "yz", 0)
    return pl.pallas_call(
        final_kernel,
        in_specs=[SMEM] + [VMEM] * 4,
        out_specs=VMEM,
        out_shape=shapes(*whole),
        compiler_params=grant(4),
        name="final",
    )(contrast, own, own_sum, far_sum, near_sum)


def solution(mesh):
    return jax.shard_map(
        per_device,
        mesh=mesh,
        in_specs=(
            P("gx", "yz", None),
            P(),
            P("gx", "yz", None),
            P("gx", "yz", None),
            P("gx", "yz"),
            P(),
            P(),
        ),
        out_specs=P("gx", "yz", None, None),
        check_vma=False,
    )
```

```python
import functools

import jax
import jax.numpy as jnp
from jax import lax
from jax.experimental import pallas as pl
from jax.experimental.pallas import tpu as pltpu
from jax.sharding import PartitionSpec as P

SLOTS = 8
NGRP = 8
REACH = 3
NCLASS = 4
ITERS = 3
BF16 = jnp.bfloat16
F32 = jnp.float32


def moved(value, axis, steps):
    count = lax.axis_size(axis)
    pairs = [(source, (source + steps) % count) for source in range(count)]
    return lax.ppermute(value, axis, pairs)


def swapped(value, axis, first):
    count = lax.axis_size(axis)
    pairs = [(k, (((k - first) ^ 1) + first) % count) for k in range(count)]
    return lax.ppermute(value, axis, pairs)


def scale_of(classes, contrast_ref):
    value = jnp.full(classes.shape, contrast_ref[0], F32)
    for k in range(1, NCLASS):
        value = jnp.where(classes == k, contrast_ref[k], value)
    return jnp.sqrt(value)


def split(value):
    high = value.astype(BF16)
    return high, (value - high.astype(F32)).astype(BF16)


def product(left, right):
    return jnp.dot(left, right, preferred_element_type=F32)


def group_ones(width, group):
    row = lax.broadcasted_iota(jnp.int32, (width, width), 0) // group
    col = lax.broadcasted_iota(jnp.int32, (width, width), 1) // group
    return jnp.where(row == col, 1.0, 0.0).astype(BF16)


def places_of(index_x, index_y, places, row_count, col_count):
    block = (index_y >= col_count).astype(jnp.int32) + (index_y >= 2 * col_count)
    col = index_y - block * col_count
    deep = 2 * REACH
    return jnp.where(
        index_x < 0,
        places[3] + (block * deep + index_x + deep) * col_count + col,
        jnp.where(
            index_x >= row_count,
            places[4] + (block * deep + index_x - row_count) * col_count + col,
            (block * row_count + index_x) * col_count + col,
        ),
    )


def sides(near_ref, far_ref):
    even = lax.axis_index("yz") % 2 == 0
    near, far = near_ref[...], far_ref[...]
    return jnp.where(even, far, near), jnp.where(even, near, far)


def prepare_kernel(
    shift_x_ref, shift_y_ref, extent_ref, classes_ref, stiffness_ref,
    own_out, info_out, down_out, up_out, high_ref, low_ref,
    shift_x, shift_y, extent, landing, arrived, *, places,
):
    parts, part = landing.shape[:2]
    small = 64

    def copy(k):
        return pltpu.make_async_copy(
            stiffness_ref.at[pl.ds(k * part, part), :], landing.at[k], arrived.at[k]
        )

    others = [
        pltpu.make_async_copy(source, target, arrived.at[parts + k])
        for k, (source, target) in enumerate((
            (shift_x_ref, shift_x), (shift_y_ref, shift_y), (extent_ref, extent),
            (classes_ref, own_out),
        ))
    ]
    for other in others:
        other.start()
    for k in range(parts):
        copy(k).start()
    for other in others:
        other.wait()
    col_count, row_count = extent.shape
    shape = shift_x.shape
    slot = lax.broadcasted_iota(jnp.int32, shape, 0) + 1
    index_x = lax.broadcasted_iota(jnp.int32, shape, 2) + shift_x[...]
    index_y = lax.broadcasted_iota(jnp.int32, shape, 1) + shift_y[...] + col_count
    live = slot < extent[...][None]
    for out, move in ((info_out, 0), (down_out, -row_count), (up_out, row_count)):
        place = places_of(index_x + move, index_y, places, row_count, col_count)
        out[0] = extent[...]
        out[1:] = jnp.where(live, place, places[5])
    for k in range(parts):
        copy(k).wait()

        def step(j, carry):
            lines = pl.ds(pl.multiple_of(k * part + j * small, small), small)
            source = pl.ds(pl.multiple_of(j * small, small), small)
            high_ref[lines, :], low_ref[lines, :] = split(landing[k, source, :])
            return carry

        lax.fori_loop(0, part // small, step, 0)


def pack_kernel(far_ref, near_ref, own_ref, down_ref, up_ref, last_out, first_out, *, bound):
    left, right = sides(near_ref, far_ref)
    deep = 2 * REACH
    for k, block in enumerate((left, own_ref[...], right)):
        lines = slice(k * deep, (k + 1) * deep)
        last_out[lines] = block[block.shape[0] - deep:]
        first_out[lines] = block[:deep]
    for info_ref, out in ((down_ref, last_out), (up_ref, first_out)):
        places = info_ref[1:]
        reached = jnp.max((places < bound).astype(jnp.int32), axis=0)
        head = 3 * deep
        count = info_ref.shape[2]
        out[head:] = jnp.zeros((out.shape[0] - head,) + out.shape[1:], jnp.int32)
        out[head, :, :count] = info_ref[0] * reached
        out[head + 1:, :, :count] = places


def solve_kernel(
    info_ref, contrast_ref, near_ref, own_ref, far_ref, above_ref, below_ref, coarse_ref,
    high_ref, low_ref,
    own_out, far_out, near_out, inverse_out,
    scales, rows, start, spread, value, high, low, picture, weighted_high, weighted_low, total,
    ranks, *, row_count, col_count, dof, places,
):
    slots = SLOTS
    patches = row_count * col_count
    columns = coarse_ref.shape[0]
    own_place, bound, empty = places[1], places[3], places[5]
    deep = 2 * REACH
    ones = group_ones(2 * dof, dof // NGRP)
    small = ones[:dof, :dof]
    scales[...] = jnp.full(scales.shape, 1.0, F32)
    left, right = sides(near_ref, far_ref)
    for place, block in zip(places, (left, own_ref[...], right)):
        scales[pl.ds(place, patches), :] = scale_of(block, contrast_ref)
    for place, block in zip(places[3:], (above_ref, below_ref)):
        for x in range(3 * deep):
            scales[pl.ds(place + x * col_count, col_count), :] = scale_of(block[x], contrast_ref)
    inverse = 1.0 / scales[...]
    first, second = split(inverse * inverse)
    weight = product(first, small) + product(second, small)
    rows[...] = inverse * lax.rsqrt(weight)
    inverse_out[...] = inverse[own_place:own_place + patches].reshape(inverse_out.shape)
    rows[pl.ds(empty, 8), :] = jnp.zeros((8, dof), F32)

    elements = [(r, y) for r in range(row_count + 2 * REACH) for y in range(col_count)]

    def first_place(r, y):
        x = r - REACH
        if x < 0:
            return places[3] + (deep + x + deep) * col_count + y
        if x >= row_count:
            return places[4] + (deep + x - row_count) * col_count + y
        return own_place + x * col_count + y

    width = 6
    half = 5

    def counted(extent, counters):
        late = extent >= half
        shift = jnp.where(late, extent - half, extent) * width
        step = jnp.left_shift(jnp.int32(1), shift)
        counter = jnp.where(late, counters[1], counters[0])
        held = jnp.bitwise_and(jnp.right_shift(counter, shift), (1 << width) - 1)
        none = jnp.int32(0)
        return held, (
            counters[0] + jnp.where(late, none, step), counters[1] + jnp.where(late, step, none)
        )

    counters = (jnp.int32(0), jnp.int32(0))
    for r, y in elements:
        _, counters = counted(info_ref[0, y, r], counters)
    starts = [jnp.int32(0), jnp.int32(0)]
    longer = [None] * (slots + 1)
    before = jnp.int32(0)
    for extent in range(slots, -1, -1):
        part, shift = divmod(extent, half)
        longer[extent] = before
        starts[part] = starts[part] + jnp.left_shift(before, shift * width)
        number = jnp.right_shift(counters[part], shift * width)
        before = before + jnp.bitwise_and(number, (1 << width) - 1)
    counters = tuple(starts)
    for p, (r, y) in enumerate(elements):
        rank, counters = counted(info_ref[0, y, r], counters)
        ranks[p] = rank
    for p, (r, y) in enumerate(elements):
        lines = pl.ds(pl.multiple_of(ranks[p] * columns, columns), columns)
        place = first_place(r, y)
        start[lines, :] = scales[place:place + 1, :] * coarse_ref[...]
        for k in range(slots):
            row = rows[pl.ds(place if k == 0 else info_ref[k, y, r], 1), :]
            spread[lines, k * dof:(k + 1) * dof] = jnp.broadcast_to(row, (columns, dof))

    block_rows = high.shape[1]
    pair = 2 * dof
    wide = 2 * pair

    def solve_block(b, pairs):
        lines = pl.ds(pl.multiple_of(b * block_rows, block_rows), block_rows)
        active = pairs * pair
        begin = start[lines, :]
        begin_high, begin_low = split(begin)
        for iteration in range(ITERS):
            for base in range(0, active, wide):
                lanes = slice(base, min(base + wide, active))
                if iteration == 0:
                    image = (
                        product(begin_high, high_ref[:dof, lanes])
                        + product(begin_high, low_ref[:dof, lanes])
                        + product(begin_low, high_ref[:dof, lanes])
                    )
                else:
                    source = (iteration - 1) % 2
                    image = (
                        product(high[source, :, :active], high_ref[:active, lanes])
                        + product(high[source, :, :active], low_ref[:active, lanes])
                        + product(low[source, :, :active], high_ref[:active, lanes])
                    )
                picture[:, lanes] = image
                first, second = split(spread[lines, lanes] * image)
                weighted_high[:, lanes] = first
                weighted_low[:, lanes] = second
            for base in range(0, active, pair):
                lanes = slice(base, base + pair)
                factor = spread[lines, lanes]
                mean = product(weighted_high[:, lanes], ones)
                mean = mean + product(weighted_low[:, lanes], ones)
                change = jnp.where(factor > 0.0, picture[:, lanes] - factor * mean, 0.0)
                result = -change if iteration == 0 else value[lines, lanes] - change
                value[lines, lanes] = result
                if iteration < ITERS - 1:
                    if base == 0:
                        result = jnp.concatenate(
                            [result[:, :dof] + begin, result[:, dof:]], axis=1
                        )
                    first, second = split(result)
                    high[iteration % 2, :, lanes] = first
                    low[iteration % 2, :, lanes] = second

    def solve_step(b, carry):
        passed = b * (block_rows // columns)
        pairs = jnp.int32(0)
        for k in range(slots // 2):
            pairs = pairs + jnp.where(longer[2 * k] > passed, 1, 0)
        for k in range(1, slots // 2 + 1):
            pl.when(pairs == k)(functools.partial(solve_block, b, k))
        return carry

    lax.fori_loop(0, spread.shape[0] // block_rows, solve_step, 0)

    total[...] = jnp.zeros(total.shape, F32)

    def result_of(p, k):
        lines = pl.ds(pl.multiple_of(ranks[p] * columns, columns), columns)
        return value[lines, k * dof:(k + 1) * dof]

    for p in range(patches):
        total[0, own_place + p] = result_of(p + REACH * col_count, 0)
    count = len(elements) // 2
    for q in range(count):
        sums = []
        for part in range(2):
            p = q + part * count
            r, y = elements[p]
            for k in range(1, slots):
                spot = jnp.minimum(info_ref[k, y, r], bound)
                sums.append((part, spot, total[part, spot] + result_of(p, k)))
        for part, spot, entry in sums:
            total[part, spot] = entry
    total[0] = total[0] + total[1]
    total = total.at[0]
    own_out[...] = total[pl.ds(own_place, patches)].reshape(own_out.shape)

    def store_sides(left_out, right_out):
        for x in range(row_count):
            for y in range(REACH):
                left_out[x, y] = total[places[0] + x * col_count + y + col_count - REACH]
                right_out[x, y] = total[places[2] + x * col_count + y]

    even = lax.axis_index("yz") % 2 == 0
    pl.when(even)(lambda: store_sides(far_out, near_out))
    pl.when(jnp.logical_not(even))(lambda: store_sides(near_out, far_out))


def final_kernel(inverse_ref, own_ref, far_ref, near_ref, out):
    count = own_ref.shape[1]
    reach = near_ref.shape[1]
    from_left, from_right = sides(near_ref, far_ref)
    out[...] = own_ref[...]
    out[:, count - reach:] = out[:, count - reach:] + from_right
    out[:, :reach] = out[:, :reach] + from_left
    out[...] = out[...] * inverse_ref[...][:, :, None, :]


SMEM = pl.BlockSpec(memory_space=pltpu.SMEM)
VMEM = pl.BlockSpec(memory_space=pltpu.VMEM)


def grant(mebibytes):
    return pltpu.CompilerParams(vmem_limit_bytes=mebibytes * 1024 * 1024)


def shapes(*dims):
    return jax.ShapeDtypeStruct(dims, F32)


def per_device(classes, contrast, shift_x, shift_y, extent, coarse_basis, stiffness):
    row_count, col_count, dof = classes.shape
    columns = coarse_basis.shape[0]
    order = SLOTS * dof
    patches = row_count * col_count
    edge = 3 * 2 * REACH * col_count
    places = [0, patches, 2 * patches, 3 * patches, 3 * patches + edge, 3 * patches + 2 * edge]
    empty = places[5]

    far = swapped(classes, "yz", 1)
    near = swapped(classes, "yz", 0)

    stiff = jax.ShapeDtypeStruct((order, order), BF16)
    ends = jax.ShapeDtypeStruct((SLOTS, col_count, row_count), jnp.int32)
    parts = 8
    turned = (SLOTS - 1, col_count, row_count)
    sources = (
        shift_x.transpose(2, 1, 0), shift_y.transpose(2, 1, 0), extent.T, classes, stiffness
    )
    own, info, down, up, stiff_high, stiff_low = pl.pallas_call(
        functools.partial(prepare_kernel, places=places),
        in_specs=[pl.BlockSpec(memory_space=pltpu.HBM)] * 5,
        out_specs=[VMEM] * 6,
        out_shape=[
            jax.ShapeDtypeStruct(classes.shape, jnp.int32), ends, ends, ends, stiff, stiff
        ],
        scratch_shapes=[
            pltpu.VMEM(turned, jnp.int32),
            pltpu.VMEM(turned, jnp.int32),
            pltpu.VMEM(turned[1:], jnp.int32),
            pltpu.VMEM((parts, order // parts, order), F32),
            pltpu.SemaphoreType.DMA((parts + 4,)),
        ],
        compiler_params=grant(8),
        cost_estimate=pl.CostEstimate(
            flops=2 * order * order, bytes_accessed=8 * order * order, transcendentals=0
        ),
        name="prepare",
    )(*(pltpu.with_memory_space_constraint(source, pltpu.HBM) for source in sources))
    far, near, own, stiff_high, stiff_low, info, down, up = lax.optimization_barrier(
        (far, near, own, stiff_high, stiff_low, info, down, up)
    )
    head = 3 * 2 * REACH
    halo = jax.ShapeDtypeStruct((head + SLOTS, col_count, dof), jnp.int32)
    last_rows, first_rows = pl.pallas_call(
        functools.partial(pack_kernel, bound=places[3]),
        in_specs=[VMEM] * 5,
        out_specs=[VMEM] * 2,
        out_shape=[halo, halo],
        compiler_params=grant(4),
        name="pack",
    )(far, near, own, down, up)
    above = moved(last_rows, "gx", 1)
    below = moved(first_rows, "gx", -1)

    info = jnp.concatenate(
        [above[head:, :, row_count - REACH:row_count], info, below[head:, :, :REACH]], axis=2
    )
    whole = (row_count, col_count, columns, dof)
    side = shapes(row_count, REACH, columns, dof)
    total_rows = (row_count + 2 * REACH) * col_count * columns
    block_rows = total_rows // 2
    own_sum, far_sum, near_sum, inverse = pl.pallas_call(
        functools.partial(
            solve_kernel, row_count=row_count, col_count=col_count, dof=dof, places=places
        ),
        in_specs=[SMEM, SMEM] + [VMEM] * 8,
        out_specs=[VMEM] * 4,
        out_shape=[shapes(*whole), side, side, shapes(row_count, col_count, dof)],
        scratch_shapes=[
            pltpu.VMEM((empty + 8, dof), F32),
            pltpu.VMEM((empty + 8, dof), F32),
            pltpu.VMEM((total_rows, dof), F32),
            pltpu.VMEM((total_rows, order), F32),
            pltpu.VMEM((total_rows, order), F32),
            pltpu.VMEM((2, block_rows, order), BF16),
            pltpu.VMEM((2, block_rows, order), BF16),
            pltpu.VMEM((block_rows, order), F32),
            pltpu.VMEM((block_rows, order), BF16),
            pltpu.VMEM((block_rows, order), BF16),
            pltpu.VMEM((2, places[3] + 1, columns, dof), F32),
            pltpu.SMEM((64,), jnp.int32),
        ],
        compiler_params=grant(16),
        name="solve",
    )(
        info, contrast, near.reshape(patches, dof), own.reshape(patches, dof),
        far.reshape(patches, dof), above, below, coarse_basis, stiff_high, stiff_low,
    )
    far_sum = swapped(far_sum, "yz", 1)
    near_sum = swapped(near_sum, "yz", 0)
    return pl.pallas_call(
        final_kernel,
        in_specs=[VMEM] * 4,
        out_specs=VMEM,
        out_shape=shapes(*whole),
        compiler_params=grant(4),
        name="final",
    )(inverse, own_sum, far_sum, near_sum)


def solution(mesh):
    return jax.shard_map(
        per_device,
        mesh=mesh,
        in_specs=(
            P("gx", "yz", None),
            P(),
            P("gx", "yz", None),
            P("gx", "yz", None),
            P("gx", "yz"),
            P(),
            P(),
        ),
        out_specs=P("gx", "yz", None, None),
        check_vma=False,
    )
```

```python
import functools

import jax
import jax.numpy as jnp
from jax import lax
from jax.experimental import pallas as pl
from jax.experimental.pallas import tpu as pltpu
from jax.sharding import PartitionSpec as P

SLOTS = 8
NGRP = 8
REACH = 3
NCLASS = 4
ITERS = 3
BF16 = jnp.bfloat16
F32 = jnp.float32


def moved(value, axis, steps):
    count = lax.axis_size(axis)
    pairs = [(source, (source + steps) % count) for source in range(count)]
    return lax.ppermute(value, axis, pairs)


def swapped(value, axis, first):
    count = lax.axis_size(axis)
    pairs = [(k, (((k - first) ^ 1) + first) % count) for k in range(count)]
    return lax.ppermute(value, axis, pairs)


def scale_of(classes, contrast_ref):
    value = jnp.full(classes.shape, contrast_ref[0], F32)
    for k in range(1, NCLASS):
        value = jnp.where(classes == k, contrast_ref[k], value)
    return jnp.sqrt(value)


def split(value):
    high = value.astype(BF16)
    return high, (value - high.astype(F32)).astype(BF16)


def product(left, right):
    return jnp.dot(left, right, preferred_element_type=F32)


def group_ones(width, group):
    row = lax.broadcasted_iota(jnp.int32, (width, width), 0) // group
    col = lax.broadcasted_iota(jnp.int32, (width, width), 1) // group
    return jnp.where(row == col, 1.0, 0.0).astype(BF16)


def places_of(index_x, index_y, places, row_count, col_count):
    block = (index_y >= col_count).astype(jnp.int32) + (index_y >= 2 * col_count)
    col = index_y - block * col_count
    deep = 2 * REACH
    return jnp.where(
        index_x < 0,
        places[3] + (block * deep + index_x + deep) * col_count + col,
        jnp.where(
            index_x >= row_count,
            places[4] + (block * deep + index_x - row_count) * col_count + col,
            (block * row_count + index_x) * col_count + col,
        ),
    )


def sides(near_ref, far_ref):
    even = lax.axis_index("yz") % 2 == 0
    near, far = near_ref[...], far_ref[...]
    return jnp.where(even, far, near), jnp.where(even, near, far)


def prepare_kernel(
    shift_x_ref, shift_y_ref, extent_ref, classes_ref, stiffness_ref,
    own_out, info_out, down_out, up_out, high_ref, low_ref,
    shift_x, shift_y, extent, landing, arrived, *, places,
):
    parts, part = landing.shape[:2]
    small = 64

    def copy(k):
        return pltpu.make_async_copy(
            stiffness_ref.at[pl.ds(k * part, part), :], landing.at[k], arrived.at[k]
        )

    others = [
        pltpu.make_async_copy(source, target, arrived.at[parts + k])
        for k, (source, target) in enumerate((
            (shift_x_ref, shift_x), (shift_y_ref, shift_y), (extent_ref, extent),
            (classes_ref, own_out),
        ))
    ]
    for other in others:
        other.start()
    for k in range(parts):
        copy(k).start()
    for other in others:
        other.wait()
    col_count, row_count = extent.shape
    shape = shift_x.shape
    slot = lax.broadcasted_iota(jnp.int32, shape, 0) + 1
    index_x = lax.broadcasted_iota(jnp.int32, shape, 2) + shift_x[...]
    index_y = lax.broadcasted_iota(jnp.int32, shape, 1) + shift_y[...] + col_count
    live = slot < extent[...][None]
    for out, move in ((info_out, 0), (down_out, -row_count), (up_out, row_count)):
        place = places_of(index_x + move, index_y, places, row_count, col_count)
        out[0] = extent[...]
        out[1:] = jnp.where(live, place, places[5])
    for k in range(parts):
        copy(k).wait()

        def step(j, carry):
            lines = pl.ds(pl.multiple_of(k * part + j * small, small), small)
            source = pl.ds(pl.multiple_of(j * small, small), small)
            high_ref[lines, :], low_ref[lines, :] = split(landing[k, source, :])
            return carry

        lax.fori_loop(0, part // small, step, 0)


def pack_kernel(far_ref, near_ref, own_ref, down_ref, up_ref, last_out, first_out, *, bound):
    left, right = sides(near_ref, far_ref)
    deep = 2 * REACH
    for k, block in enumerate((left, own_ref[...], right)):
        lines = slice(k * deep, (k + 1) * deep)
        last_out[lines] = block[block.shape[0] - deep:]
        first_out[lines] = block[:deep]
    for info_ref, out in ((down_ref, last_out), (up_ref, first_out)):
        places = info_ref[1:]
        reached = jnp.max((places < bound).astype(jnp.int32), axis=0)
        head = 3 * deep
        count = info_ref.shape[2]
        out[head:] = jnp.zeros((out.shape[0] - head,) + out.shape[1:], jnp.int32)
        out[head, :, :count] = info_ref[0] * reached
        out[head + 1:, :, :count] = places


def solve_kernel(
    info_ref, contrast_ref, near_ref, own_ref, far_ref, above_ref, below_ref, coarse_ref,
    high_ref, low_ref,
    own_out, far_out, near_out, inverse_out,
    scales, rows, start, spread, value, high, low, picture, weighted_high, weighted_low, total,
    ranks, *, row_count, col_count, dof, places,
):
    slots = SLOTS
    patches = row_count * col_count
    columns = coarse_ref.shape[0]
    own_place, bound, empty = places[1], places[3], places[5]
    deep = 2 * REACH
    ones = group_ones(2 * dof, dof // NGRP)
    small = ones[:dof, :dof]
    scales[...] = jnp.full(scales.shape, 1.0, F32)
    left, right = sides(near_ref, far_ref)
    for place, block in zip(places, (left, own_ref[...], right)):
        scales[pl.ds(place, patches), :] = scale_of(block, contrast_ref)
    for place, block in zip(places[3:], (above_ref, below_ref)):
        for x in range(3 * deep):
            scales[pl.ds(place + x * col_count, col_count), :] = scale_of(block[x], contrast_ref)
    inverse = 1.0 / scales[...]
    first, second = split(inverse * inverse)
    weight = product(first, small) + product(second, small)
    rows[...] = inverse * lax.rsqrt(weight)
    inverse_out[...] = inverse[own_place:own_place + patches].reshape(inverse_out.shape)
    rows[pl.ds(empty, 8), :] = jnp.zeros((8, dof), F32)

    elements = [(r, y) for r in range(row_count + 2 * REACH) for y in range(col_count)]

    def first_place(r, y):
        x = r - REACH
        if x < 0:
            return places[3] + (deep + x + deep) * col_count + y
        if x >= row_count:
            return places[4] + (deep + x - row_count) * col_count + y
        return own_place + x * col_count + y

    width = 6
    half = 5

    def counted(extent, counters):
        late = extent >= half
        shift = jnp.where(late, extent - half, extent) * width
        step = jnp.left_shift(jnp.int32(1), shift)
        counter = jnp.where(late, counters[1], counters[0])
        held = jnp.bitwise_and(jnp.right_shift(counter, shift), (1 << width) - 1)
        none = jnp.int32(0)
        return held, (
            counters[0] + jnp.where(late, none, step), counters[1] + jnp.where(late, step, none)
        )

    counters = (jnp.int32(0), jnp.int32(0))
    for r, y in elements:
        _, counters = counted(info_ref[0, y, r], counters)
    starts = [jnp.int32(0), jnp.int32(0)]
    longer = [None] * (slots + 1)
    before = jnp.int32(0)
    for extent in range(slots, -1, -1):
        part, shift = divmod(extent, half)
        longer[extent] = before
        starts[part] = starts[part] + jnp.left_shift(before, shift * width)
        number = jnp.right_shift(counters[part], shift * width)
        before = before + jnp.bitwise_and(number, (1 << width) - 1)
    counters = tuple(starts)
    for p, (r, y) in enumerate(elements):
        rank, counters = counted(info_ref[0, y, r], counters)
        ranks[p] = rank
    for p, (r, y) in enumerate(elements):
        lines = pl.ds(pl.multiple_of(ranks[p] * columns, columns), columns)
        place = first_place(r, y)
        start[lines, :] = scales[place:place + 1, :] * coarse_ref[...]
        for k in range(slots):
            row = rows[pl.ds(place if k == 0 else info_ref[k, y, r], 1), :]
            spread[lines, k * dof:(k + 1) * dof] = jnp.broadcast_to(row, (columns, dof))

    pair = 2 * dof
    wide = 2 * pair

    def solve_block(lines, pairs):
        inner = slice(0, lines.stop - lines.start)
        active = pairs * pair
        begin = start[lines, :]
        begin_high, begin_low = split(begin)
        for iteration in range(ITERS):
            for base in range(0, active, wide):
                lanes = slice(base, min(base + wide, active))
                if iteration == 0:
                    image = (
                        product(begin_high, high_ref[:dof, lanes])
                        + product(begin_high, low_ref[:dof, lanes])
                        + product(begin_low, high_ref[:dof, lanes])
                    )
                else:
                    source = (iteration - 1) % 2
                    image = (
                        product(high[source, inner, :active], high_ref[:active, lanes])
                        + product(high[source, inner, :active], low_ref[:active, lanes])
                        + product(low[source, inner, :active], high_ref[:active, lanes])
                    )
                picture[inner, lanes] = image
                first, second = split(spread[lines, lanes] * image)
                weighted_high[inner, lanes] = first
                weighted_low[inner, lanes] = second
            for base in range(0, active, pair):
                lanes = slice(base, base + pair)
                factor = spread[lines, lanes]
                mean = product(weighted_high[inner, lanes], ones)
                mean = mean + product(weighted_low[inner, lanes], ones)
                change = jnp.where(factor > 0.0, picture[inner, lanes] - factor * mean, 0.0)
                result = -change if iteration == 0 else value[lines, lanes] - change
                value[lines, lanes] = result
                if iteration < ITERS - 1:
                    if base == 0:
                        result = jnp.concatenate(
                            [result[:, :dof] + begin, result[:, dof:]], axis=1
                        )
                    first, second = split(result)
                    high[iteration % 2, inner, lanes] = first
                    low[iteration % 2, inner, lanes] = second

    passed = high.shape[1] // columns
    solve_block(slice(0, high.shape[1]), slots // 2)
    pairs = jnp.int32(2)
    for k in range(2, slots // 2):
        pairs = pairs + jnp.where(longer[2 * k] > passed, 1, 0)
    others = slice(high.shape[1], spread.shape[0])
    for k in range(2, slots // 2 + 1):
        pl.when(pairs == k)(functools.partial(solve_block, others, k))

    total[...] = jnp.zeros(total.shape, F32)

    def result_of(p, k):
        lines = pl.ds(pl.multiple_of(ranks[p] * columns, columns), columns)
        return value[lines, k * dof:(k + 1) * dof]

    for p in range(patches):
        total[0, own_place + p] = result_of(p + REACH * col_count, 0)
    count = len(elements) // 2
    for q in range(count):
        sums = []
        for part in range(2):
            p = q + part * count
            r, y = elements[p]
            for k in range(1, slots):
                spot = jnp.minimum(info_ref[k, y, r], bound)
                sums.append((part, spot, total[part, spot] + result_of(p, k)))
        for part, spot, entry in sums:
            total[part, spot] = entry
    total[0] = total[0] + total[1]
    total = total.at[0]
    own_out[...] = total[pl.ds(own_place, patches)].reshape(own_out.shape)

    def store_sides(left_out, right_out):
        for x in range(row_count):
            for y in range(REACH):
                left_out[x, y] = total[places[0] + x * col_count + y + col_count - REACH]
                right_out[x, y] = total[places[2] + x * col_count + y]

    even = lax.axis_index("yz") % 2 == 0
    pl.when(even)(lambda: store_sides(far_out, near_out))
    pl.when(jnp.logical_not(even))(lambda: store_sides(near_out, far_out))


def final_kernel(inverse_ref, own_ref, far_ref, near_ref, out):
    count = own_ref.shape[1]
    reach = near_ref.shape[1]
    from_left, from_right = sides(near_ref, far_ref)
    out[...] = own_ref[...]
    out[:, count - reach:] = out[:, count - reach:] + from_right
    out[:, :reach] = out[:, :reach] + from_left
    out[...] = out[...] * inverse_ref[...][:, :, None, :]


SMEM = pl.BlockSpec(memory_space=pltpu.SMEM)
VMEM = pl.BlockSpec(memory_space=pltpu.VMEM)


def grant(mebibytes):
    return pltpu.CompilerParams(vmem_limit_bytes=mebibytes * 1024 * 1024)


def shapes(*dims):
    return jax.ShapeDtypeStruct(dims, F32)


def per_device(classes, contrast, shift_x, shift_y, extent, coarse_basis, stiffness):
    row_count, col_count, dof = classes.shape
    columns = coarse_basis.shape[0]
    order = SLOTS * dof
    patches = row_count * col_count
    edge = 3 * 2 * REACH * col_count
    places = [0, patches, 2 * patches, 3 * patches, 3 * patches + edge, 3 * patches + 2 * edge]
    empty = places[5]

    far = swapped(classes, "yz", 1)
    near = swapped(classes, "yz", 0)

    stiff = jax.ShapeDtypeStruct((order, order), BF16)
    ends = jax.ShapeDtypeStruct((SLOTS, col_count, row_count), jnp.int32)
    parts = 8
    turned = (SLOTS - 1, col_count, row_count)
    sources = (
        shift_x.transpose(2, 1, 0), shift_y.transpose(2, 1, 0), extent.T, classes, stiffness
    )
    own, info, down, up, stiff_high, stiff_low = pl.pallas_call(
        functools.partial(prepare_kernel, places=places),
        in_specs=[pl.BlockSpec(memory_space=pltpu.HBM)] * 5,
        out_specs=[VMEM] * 6,
        out_shape=[
            jax.ShapeDtypeStruct(classes.shape, jnp.int32), ends, ends, ends, stiff, stiff
        ],
        scratch_shapes=[
            pltpu.VMEM(turned, jnp.int32),
            pltpu.VMEM(turned, jnp.int32),
            pltpu.VMEM(turned[1:], jnp.int32),
            pltpu.VMEM((parts, order // parts, order), F32),
            pltpu.SemaphoreType.DMA((parts + 4,)),
        ],
        compiler_params=grant(8),
        cost_estimate=pl.CostEstimate(
            flops=2 * order * order, bytes_accessed=8 * order * order, transcendentals=0
        ),
        name="prepare",
    )(*(pltpu.with_memory_space_constraint(source, pltpu.HBM) for source in sources))
    far, near, own, stiff_high, stiff_low, info, down, up = lax.optimization_barrier(
        (far, near, own, stiff_high, stiff_low, info, down, up)
    )
    head = 3 * 2 * REACH
    halo = jax.ShapeDtypeStruct((head + SLOTS, col_count, dof), jnp.int32)
    last_rows, first_rows = pl.pallas_call(
        functools.partial(pack_kernel, bound=places[3]),
        in_specs=[VMEM] * 5,
        out_specs=[VMEM] * 2,
        out_shape=[halo, halo],
        compiler_params=grant(4),
        name="pack",
    )(far, near, own, down, up)
    above = moved(last_rows, "gx", 1)
    below = moved(first_rows, "gx", -1)

    info = jnp.concatenate(
        [above[head:, :, row_count - REACH:row_count], info, below[head:, :, :REACH]], axis=2
    )
    whole = (row_count, col_count, columns, dof)
    side = shapes(row_count, REACH, columns, dof)
    total_rows = (row_count + 2 * REACH) * col_count * columns
    block_rows = 32 * columns
    own_sum, far_sum, near_sum, inverse = pl.pallas_call(
        functools.partial(
            solve_kernel, row_count=row_count, col_count=col_count, dof=dof, places=places
        ),
        in_specs=[SMEM, SMEM] + [VMEM] * 8,
        out_specs=[VMEM] * 4,
        out_shape=[shapes(*whole), side, side, shapes(row_count, col_count, dof)],
        scratch_shapes=[
            pltpu.VMEM((empty + 8, dof), F32),
            pltpu.VMEM((empty + 8, dof), F32),
            pltpu.VMEM((total_rows, dof), F32),
            pltpu.VMEM((total_rows, order), F32),
            pltpu.VMEM((total_rows, order), F32),
            pltpu.VMEM((2, block_rows, order), BF16),
            pltpu.VMEM((2, block_rows, order), BF16),
            pltpu.VMEM((block_rows, order), F32),
            pltpu.VMEM((block_rows, order), BF16),
            pltpu.VMEM((block_rows, order), BF16),
            pltpu.VMEM((2, places[3] + 1, columns, dof), F32),
            pltpu.SMEM((64,), jnp.int32),
        ],
        compiler_params=grant(16),
        name="solve",
    )(
        info, contrast, near.reshape(patches, dof), own.reshape(patches, dof),
        far.reshape(patches, dof), above, below, coarse_basis, stiff_high, stiff_low,
    )
    far_sum = swapped(far_sum, "yz", 1)
    near_sum = swapped(near_sum, "yz", 0)
    return pl.pallas_call(
        final_kernel,
        in_specs=[VMEM] * 4,
        out_specs=VMEM,
        out_shape=shapes(*whole),
        compiler_params=grant(4),
        name="final",
    )(inverse, own_sum, far_sum, near_sum)


def solution(mesh):
    return jax.shard_map(
        per_device,
        mesh=mesh,
        in_specs=(
            P("gx", "yz", None),
            P(),
            P("gx", "yz", None),
            P("gx", "yz", None),
            P("gx", "yz"),
            P(),
            P(),
        ),
        out_specs=P("gx", "yz", None, None),
        check_vma=False,
    )
```

```python
import functools

import jax
import jax.numpy as jnp
from jax import lax
from jax.experimental import pallas as pl
from jax.experimental.pallas import tpu as pltpu
from jax.sharding import PartitionSpec as P

SLOTS = 8
NGRP = 8
REACH = 3
NCLASS = 4
ITERS = 3
BF16 = jnp.bfloat16
F32 = jnp.float32


def moved(value, axis, steps):
    count = lax.axis_size(axis)
    pairs = [(source, (source + steps) % count) for source in range(count)]
    return lax.ppermute(value, axis, pairs)


def swapped(value, axis, first):
    count = lax.axis_size(axis)
    pairs = [(k, (((k - first) ^ 1) + first) % count) for k in range(count)]
    return lax.ppermute(value, axis, pairs)


def scale_of(classes, contrast_ref):
    value = jnp.full(classes.shape, contrast_ref[0], F32)
    for k in range(1, NCLASS):
        value = jnp.where(classes == k, contrast_ref[k], value)
    return jnp.sqrt(value)


def split(value):
    high = value.astype(BF16)
    return high, (value - high.astype(F32)).astype(BF16)


def product(left, right):
    return jnp.dot(left, right, preferred_element_type=F32)


def group_ones(width, group):
    row = lax.broadcasted_iota(jnp.int32, (width, width), 0) // group
    col = lax.broadcasted_iota(jnp.int32, (width, width), 1) // group
    return jnp.where(row == col, 1.0, 0.0).astype(BF16)


def places_of(index_x, index_y, places, row_count, col_count):
    block = (index_y >= col_count).astype(jnp.int32) + (index_y >= 2 * col_count)
    col = index_y - block * col_count
    deep = 2 * REACH
    return jnp.where(
        index_x < 0,
        places[3] + (block * deep + index_x + deep) * col_count + col,
        jnp.where(
            index_x >= row_count,
            places[4] + (block * deep + index_x - row_count) * col_count + col,
            (block * row_count + index_x) * col_count + col,
        ),
    )


def sides(near_ref, far_ref):
    even = lax.axis_index("yz") % 2 == 0
    near, far = near_ref[...], far_ref[...]
    return jnp.where(even, far, near), jnp.where(even, near, far)


def prepare_kernel(
    shift_x_ref, shift_y_ref, extent_ref, classes_ref, stiffness_ref,
    own_out, info_out, down_out, up_out, high_ref, low_ref,
    shift_x, shift_y, extent, landing, arrived, *, places,
):
    parts, part = landing.shape[:2]
    small = 64

    def copy(k):
        return pltpu.make_async_copy(
            stiffness_ref.at[pl.ds(k * part, part), :], landing.at[k], arrived.at[k]
        )

    others = [
        pltpu.make_async_copy(source, target, arrived.at[parts + k])
        for k, (source, target) in enumerate((
            (shift_x_ref, shift_x), (shift_y_ref, shift_y), (extent_ref, extent),
            (classes_ref, own_out),
        ))
    ]
    for other in others:
        other.start()
    for k in range(parts):
        copy(k).start()
    for other in others:
        other.wait()
    col_count, row_count = extent.shape
    shape = shift_x.shape
    slot = lax.broadcasted_iota(jnp.int32, shape, 0) + 1
    index_x = lax.broadcasted_iota(jnp.int32, shape, 2) + shift_x[...]
    index_y = lax.broadcasted_iota(jnp.int32, shape, 1) + shift_y[...] + col_count
    live = slot < extent[...][None]
    for out, move in ((info_out, 0), (down_out, -row_count), (up_out, row_count)):
        place = places_of(index_x + move, index_y, places, row_count, col_count)
        out[0] = extent[...]
        out[1:] = jnp.where(live, place, places[5])
    for k in range(parts):
        copy(k).wait()

        def step(j, carry):
            lines = pl.ds(pl.multiple_of(k * part + j * small, small), small)
            source = pl.ds(pl.multiple_of(j * small, small), small)
            high_ref[lines, :], low_ref[lines, :] = split(landing[k, source, :])
            return carry

        lax.fori_loop(0, part // small, step, 0)


def pack_kernel(far_ref, near_ref, own_ref, down_ref, up_ref, last_out, first_out, *, bound):
    left, right = sides(near_ref, far_ref)
    deep = 2 * REACH
    for k, block in enumerate((left, own_ref[...], right)):
        lines = slice(k * deep, (k + 1) * deep)
        last_out[lines] = block[block.shape[0] - deep:]
        first_out[lines] = block[:deep]
    for info_ref, out in ((down_ref, last_out), (up_ref, first_out)):
        places = info_ref[1:]
        reached = jnp.max((places < bound).astype(jnp.int32), axis=0)
        head = 3 * deep
        count = info_ref.shape[2]
        out[head:] = jnp.zeros((out.shape[0] - head,) + out.shape[1:], jnp.int32)
        out[head, :, :count] = info_ref[0] * reached
        out[head + 1:, :, :count] = places


def solve_kernel(
    info_ref, contrast_ref, near_ref, own_ref, far_ref, above_ref, below_ref, coarse_ref,
    high_ref, low_ref,
    own_out, far_out, near_out, inverse_out,
    scales, rows, start, spread, value, high, low, picture, weighted_high, weighted_low, total,
    ranks, *, row_count, col_count, dof, places,
):
    slots = SLOTS
    patches = row_count * col_count
    columns = coarse_ref.shape[0]
    own_place, bound, empty = places[1], places[3], places[5]
    deep = 2 * REACH
    ones = group_ones(2 * dof, dof // NGRP)
    small = ones[:dof, :dof]
    scales[...] = jnp.full(scales.shape, 1.0, F32)
    left, right = sides(near_ref, far_ref)
    for place, block in zip(places, (left, own_ref[...], right)):
        scales[pl.ds(place, patches), :] = scale_of(block, contrast_ref)
    for place, block in zip(places[3:], (above_ref, below_ref)):
        for x in range(3 * deep):
            scales[pl.ds(place + x * col_count, col_count), :] = scale_of(block[x], contrast_ref)
    inverse = 1.0 / scales[...]
    first, second = split(inverse * inverse)
    weight = product(first, small) + product(second, small)
    rows[...] = inverse * lax.rsqrt(weight)
    inverse_out[...] = inverse[own_place:own_place + patches].reshape(inverse_out.shape)
    rows[pl.ds(empty, 8), :] = jnp.zeros((8, dof), F32)

    elements = [(r, y) for r in range(row_count + 2 * REACH) for y in range(col_count)]

    def first_place(r, y):
        x = r - REACH
        if x < 0:
            return places[3] + (deep + x + deep) * col_count + y
        if x >= row_count:
            return places[4] + (deep + x - row_count) * col_count + y
        return own_place + x * col_count + y

    width = 6
    half = 5

    def counted(extent, counters):
        late = extent >= half
        shift = jnp.where(late, extent - half, extent) * width
        step = jnp.left_shift(jnp.int32(1), shift)
        counter = jnp.where(late, counters[1], counters[0])
        held = jnp.bitwise_and(jnp.right_shift(counter, shift), (1 << width) - 1)
        none = jnp.int32(0)
        return held, (
            counters[0] + jnp.where(late, none, step), counters[1] + jnp.where(late, step, none)
        )

    counters = (jnp.int32(0), jnp.int32(0))
    for r, y in elements:
        _, counters = counted(info_ref[0, y, r], counters)
    starts = [jnp.int32(0), jnp.int32(0)]
    longer = [None] * (slots + 1)
    before = jnp.int32(0)
    for extent in range(slots, -1, -1):
        part, shift = divmod(extent, half)
        longer[extent] = before
        starts[part] = starts[part] + jnp.left_shift(before, shift * width)
        number = jnp.right_shift(counters[part], shift * width)
        before = before + jnp.bitwise_and(number, (1 << width) - 1)
    counters = tuple(starts)
    for p, (r, y) in enumerate(elements):
        rank, counters = counted(info_ref[0, y, r], counters)
        ranks[p] = rank
    for p, (r, y) in enumerate(elements):
        lines = pl.ds(pl.multiple_of(ranks[p] * columns, columns), columns)
        place = first_place(r, y)
        start[lines, :] = scales[place:place + 1, :] * coarse_ref[...]
        for k in range(slots):
            row = rows[pl.ds(place if k == 0 else info_ref[k, y, r], 1), :]
            spread[lines, k * dof:(k + 1) * dof] = jnp.broadcast_to(row, (columns, dof))

    pair = 2 * dof
    wide = 4 * pair

    def solve_block(lines, pairs):
        inner = slice(0, lines.stop - lines.start)
        active = pairs * pair
        begin = start[lines, :]
        begin_high, begin_low = split(begin)
        for iteration in range(ITERS):
            for base in range(0, active, wide):
                lanes = slice(base, min(base + wide, active))
                if iteration == 0:
                    image = (
                        product(begin_high, high_ref[:dof, lanes])
                        + product(begin_high, low_ref[:dof, lanes])
                        + product(begin_low, high_ref[:dof, lanes])
                    )
                else:
                    source = (iteration - 1) % 2
                    image = (
                        product(high[source, inner, :active], high_ref[:active, lanes])
                        + product(high[source, inner, :active], low_ref[:active, lanes])
                        + product(low[source, inner, :active], high_ref[:active, lanes])
                    )
                picture[inner, lanes] = image
                first, second = split(spread[lines, lanes] * image)
                weighted_high[inner, lanes] = first
                weighted_low[inner, lanes] = second
            for base in range(0, active, pair):
                lanes = slice(base, base + pair)
                factor = spread[lines, lanes]
                mean = product(weighted_high[inner, lanes], ones)
                mean = mean + product(weighted_low[inner, lanes], ones)
                change = jnp.where(factor > 0.0, picture[inner, lanes] - factor * mean, 0.0)
                result = -change if iteration == 0 else value[lines, lanes] - change
                value[lines, lanes] = result
                if iteration < ITERS - 1:
                    if base == 0:
                        result = jnp.concatenate(
                            [result[:, :dof] + begin, result[:, dof:]], axis=1
                        )
                    first, second = split(result)
                    high[iteration % 2, inner, lanes] = first
                    low[iteration % 2, inner, lanes] = second

    passed = high.shape[1] // columns
    solve_block(slice(0, high.shape[1]), slots // 2)
    pairs = jnp.int32(2)
    for k in range(2, slots // 2):
        pairs = pairs + jnp.where(longer[2 * k] > passed, 1, 0)
    others = slice(high.shape[1], spread.shape[0])
    for k in range(2, slots // 2 + 1):
        pl.when(pairs == k)(functools.partial(solve_block, others, k))

    total[...] = jnp.zeros(total.shape, F32)

    def result_of(p, k):
        lines = pl.ds(pl.multiple_of(ranks[p] * columns, columns), columns)
        return value[lines, k * dof:(k + 1) * dof]

    for p in range(patches):
        total[0, own_place + p] = result_of(p + REACH * col_count, 0)
    count = len(elements) // 2
    for q in range(count):
        sums = []
        for part in range(2):
            p = q + part * count
            r, y = elements[p]
            for k in range(1, slots):
                spot = jnp.minimum(info_ref[k, y, r], bound)
                sums.append((part, spot, total[part, spot] + result_of(p, k)))
        for part, spot, entry in sums:
            total[part, spot] = entry
    total[0] = total[0] + total[1]
    total = total.at[0]
    own_out[...] = total[pl.ds(own_place, patches)].reshape(own_out.shape)

    def store_sides(left_out, right_out):
        for x in range(row_count):
            for y in range(REACH):
                left_out[x, y] = total[places[0] + x * col_count + y + col_count - REACH]
                right_out[x, y] = total[places[2] + x * col_count + y]

    even = lax.axis_index("yz") % 2 == 0
    pl.when(even)(lambda: store_sides(far_out, near_out))
    pl.when(jnp.logical_not(even))(lambda: store_sides(near_out, far_out))


def final_kernel(inverse_ref, own_ref, far_ref, near_ref, out):
    count = own_ref.shape[1]
    reach = near_ref.shape[1]
    from_left, from_right = sides(near_ref, far_ref)
    out[...] = own_ref[...]
    out[:, count - reach:] = out[:, count - reach:] + from_right
    out[:, :reach] = out[:, :reach] + from_left
    out[...] = out[...] * inverse_ref[...][:, :, None, :]


SMEM = pl.BlockSpec(memory_space=pltpu.SMEM)
VMEM = pl.BlockSpec(memory_space=pltpu.VMEM)


def grant(mebibytes):
    return pltpu.CompilerParams(vmem_limit_bytes=mebibytes * 1024 * 1024)


def shapes(*dims):
    return jax.ShapeDtypeStruct(dims, F32)


def per_device(classes, contrast, shift_x, shift_y, extent, coarse_basis, stiffness):
    row_count, col_count, dof = classes.shape
    columns = coarse_basis.shape[0]
    order = SLOTS * dof
    patches = row_count * col_count
    edge = 3 * 2 * REACH * col_count
    places = [0, patches, 2 * patches, 3 * patches, 3 * patches + edge, 3 * patches + 2 * edge]
    empty = places[5]

    far = swapped(classes, "yz", 1)
    near = swapped(classes, "yz", 0)

    stiff = jax.ShapeDtypeStruct((order, order), BF16)
    ends = jax.ShapeDtypeStruct((SLOTS, col_count, row_count), jnp.int32)
    parts = 8
    turned = (SLOTS - 1, col_count, row_count)
    sources = (
        shift_x.transpose(2, 1, 0), shift_y.transpose(2, 1, 0), extent.T, classes, stiffness
    )
    own, info, down, up, stiff_high, stiff_low = pl.pallas_call(
        functools.partial(prepare_kernel, places=places),
        in_specs=[pl.BlockSpec(memory_space=pltpu.HBM)] * 5,
        out_specs=[VMEM] * 6,
        out_shape=[
            jax.ShapeDtypeStruct(classes.shape, jnp.int32), ends, ends, ends, stiff, stiff
        ],
        scratch_shapes=[
            pltpu.VMEM(turned, jnp.int32),
            pltpu.VMEM(turned, jnp.int32),
            pltpu.VMEM(turned[1:], jnp.int32),
            pltpu.VMEM((parts, order // parts, order), F32),
            pltpu.SemaphoreType.DMA((parts + 4,)),
        ],
        compiler_params=grant(8),
        cost_estimate=pl.CostEstimate(
            flops=2 * order * order, bytes_accessed=8 * order * order, transcendentals=0
        ),
        name="prepare",
    )(*(pltpu.with_memory_space_constraint(source, pltpu.HBM) for source in sources))
    far, near, own, stiff_high, stiff_low, info, down, up = lax.optimization_barrier(
        (far, near, own, stiff_high, stiff_low, info, down, up)
    )
    head = 3 * 2 * REACH
    halo = jax.ShapeDtypeStruct((head + SLOTS, col_count, dof), jnp.int32)
    last_rows, first_rows = pl.pallas_call(
        functools.partial(pack_kernel, bound=places[3]),
        in_specs=[VMEM] * 5,
        out_specs=[VMEM] * 2,
        out_shape=[halo, halo],
        compiler_params=grant(4),
        name="pack",
    )(far, near, own, down, up)
    above = moved(last_rows, "gx", 1)
    below = moved(first_rows, "gx", -1)

    info = jnp.concatenate(
        [above[head:, :, row_count - REACH:row_count], info, below[head:, :, :REACH]], axis=2
    )
    whole = (row_count, col_count, columns, dof)
    side = shapes(row_count, REACH, columns, dof)
    total_rows = (row_count + 2 * REACH) * col_count * columns
    block_rows = 32 * columns
    own_sum, far_sum, near_sum, inverse = pl.pallas_call(
        functools.partial(
            solve_kernel, row_count=row_count, col_count=col_count, dof=dof, places=places
        ),
        in_specs=[SMEM, SMEM] + [VMEM] * 8,
        out_specs=[VMEM] * 4,
        out_shape=[shapes(*whole), side, side, shapes(row_count, col_count, dof)],
        scratch_shapes=[
            pltpu.VMEM((empty + 8, dof), F32),
            pltpu.VMEM((empty + 8, dof), F32),
            pltpu.VMEM((total_rows, dof), F32),
            pltpu.VMEM((total_rows, order), F32),
            pltpu.VMEM((total_rows, order), F32),
            pltpu.VMEM((2, block_rows, order), BF16),
            pltpu.VMEM((2, block_rows, order), BF16),
            pltpu.VMEM((block_rows, order), F32),
            pltpu.VMEM((block_rows, order), BF16),
            pltpu.VMEM((block_rows, order), BF16),
            pltpu.VMEM((2, places[3] + 1, columns, dof), F32),
            pltpu.SMEM((64,), jnp.int32),
        ],
        compiler_params=grant(16),
        name="solve",
    )(
        info, contrast, near.reshape(patches, dof), own.reshape(patches, dof),
        far.reshape(patches, dof), above, below, coarse_basis, stiff_high, stiff_low,
    )
    far_sum = swapped(far_sum, "yz", 1)
    near_sum = swapped(near_sum, "yz", 0)
    return pl.pallas_call(
        final_kernel,
        in_specs=[VMEM] * 4,
        out_specs=VMEM,
        out_shape=shapes(*whole),
        compiler_params=grant(4),
        name="final",
    )(inverse, own_sum, far_sum, near_sum)


def solution(mesh):
    return jax.shard_map(
        per_device,
        mesh=mesh,
        in_specs=(
            P("gx", "yz", None),
            P(),
            P("gx", "yz", None),
            P("gx", "yz", None),
            P("gx", "yz"),
            P(),
            P(),
        ),
        out_specs=P("gx", "yz", None, None),
        check_vma=False,
    )
```
